128 devices in a mesh: section: 2 (over core), tp: 64 (over z, y, x).
Axes of the slice: x: 4, y: 4, z: 4, core: 2. Of those that a mesh axis runs over, the one named last changes fastest.
Arguments:
- incoming_hidden_states: bfloat16 [16, 8192], replicated, may hold values from -6 to 6
- parent_positions: int32 [16], replicated, may hold values from 0 to 15
- filled_extents: int32 [16], replicated, may hold values from 1 to 32, as said below
- stored_address_tensor: bfloat16 [2, 16, 32, 1024], P('section'), may hold values from -6 to 6
- stored_content_tensor: bfloat16 [2, 16, 32, 1024], P('section'), may hold values from -6 to 6
- layer_scale_factors: bfloat16 [2, 8192], P('section'), may hold values from 0.5 to 1.5
- question_matrix: bfloat16 [2, 8192, 8192], P('section', None, 'tp'), may hold values from -0.0625 to 0.0625
- address_content_matrix: bfloat16 [2, 8192, 2048], P('section'), may hold values from -0.0625 to 0.0625
- projection_back_matrix: bfloat16 [2, 8192, 8192], P('section', 'tp'), may hold values from -0.0625 to 0.0625
- ending_scale_factors: bfloat16 [8192], replicated, may hold values from 0.5 to 1.5
- lexicon_matrix: bfloat16 [32768, 8192], P(('section', 'tp')), may hold values from -0.1875 to 0.1875
- sampling_warmth: float32 [16], replicated, may hold values from 0.6 to 1.4
- sampling_noise: float32 [16, 32768], P(None, ('section', 'tp')), as said below
Outputs:
- new_entries: bfloat16 [2, 16, 2048], P('section', None, 'tp')
- final_hidden: bfloat16 [16, 8192], replicated
- top_score: float32 [16], replicated
- log_norm: float32 [16], replicated
The draws below stay inside these ranges and needn't reach their ends.
Inputs may be any that keep to these rules, and one draw needn't show every extreme that they name: Slot j continues old slot parent_positions[j]; an old slot may be named several times or not at all. `filled_extents`: some old slot has exactly 32 filled slots and some exactly one. `sampling_noise`: standard Gumbel noise.
All inputs are finite; a program needn't handle non-finite values.
Results may differ from the reference program's by a relative error of at most 0.013.
Values may be sent and summed in bfloat16 or wider, within the bound.
No kernel may reach another device: no remote copies, remote signals or barrier semaphores. Data moves between devices by JAX's collectives and lax.ppermute only.
A program may use at most 128 MiB of HBM per device.

```python
import jax
import jax.numpy as jnp
from jax import lax

D = 8192
HEAD = 128
KV_HEADS = 8
CACHE = 32
ALL_DECODE_LINES = 16
LAYERS = 2
Q_HEADS = 64
VOCAB = 32768


def draw_filled_extents(key, part):
    key = jax.random.fold_in(key, 11)
    first_key, second_key = jax.random.split(key)
    drawn_lengths = jax.random.randint(first_key, (ALL_DECODE_LINES,), 1, CACHE + 1)
    shuffled = jax.random.permutation(second_key, ALL_DECODE_LINES)
    drawn_lengths = drawn_lengths.at[shuffled[0]].set(CACHE).at[shuffled[1]].set(1)
    return drawn_lengths.astype(jnp.int32)


def draw_sampling_noise(key, part):
    key = jax.random.fold_in(key, 23)
    uniform_draw = jax.random.uniform(key, (ALL_DECODE_LINES, VOCAB), jnp.float32, 1e-06, 1.0 - 1e-06)
    return -jnp.log(-jnp.log(uniform_draw))


def place_ends(result, stream_key, least, top_value):
    shape = result.shape
    spot = [jax.random.randint(jax.random.fold_in(stream_key, axis), (), 0, shape[axis]) for axis in range(len(shape))]
    result = result.at[tuple(spot)].set(least)
    longest = shape.index(max(shape))
    spot[longest] = (spot[longest] + 1) % shape[longest]
    return result.at[tuple(spot)].set(top_value)


def levels(own_key, extent, shards, least, top_value):
    loudness = 1.0
    for position, parts in shards:
        draws = jax.random.uniform(jax.random.fold_in(jax.random.fold_in(own_key, 6), position), (parts,), jnp.float32, least / len(shards), top_value / len(shards))
        loudness = loudness * jnp.repeat(jnp.exp(draws), extent[position] // parts).reshape((-1,) + (1,) * (len(extent) - 1 - position))
    return loudness


def bell_draw(own_key, shape, width, limit, shards=(), held_as=jnp.bfloat16):
    level = levels(own_key, shape, shards, -0.22, 0.18) if shards else 1.0
    drawn = jax.random.normal(own_key, shape, jnp.float32) * width * level
    return jnp.minimum(jnp.maximum(drawn, -limit), limit).astype(held_as)


def setup_inputs(seed: int = 0) -> dict:
    key_list = jax.random.split(jax.random.key(seed), 14)
    incoming_hidden_states = bell_draw(key_list[0], (ALL_DECODE_LINES, D), 1.0, 6.0)
    parent_positions = place_ends(jax.random.randint(key_list[1], (ALL_DECODE_LINES,), 0, ALL_DECODE_LINES), jax.random.fold_in(key_list[1], 1), 0, ALL_DECODE_LINES - 1).astype(jnp.int32)
    filled_extents = draw_filled_extents(jax.random.fold_in(key_list[13], 71), 0)
    stored_address_tensor = bell_draw(key_list[3], (LAYERS, ALL_DECODE_LINES, CACHE, KV_HEADS * HEAD), 1.0, 6.0, ((0, 2),))
    stored_content_tensor = bell_draw(key_list[4], (LAYERS, ALL_DECODE_LINES, CACHE, KV_HEADS * HEAD), 1.0, 6.0, ((0, 2),))
    layer_scale_factors = jnp.clip(1.0 + 0.1 * jax.random.normal(key_list[5], (LAYERS, D), jnp.float32), 0.5, 1.5).astype(jnp.bfloat16)
    question_matrix = bell_draw(key_list[6], (LAYERS, D, Q_HEADS * HEAD), D ** -0.5, 0.0625, ((0, 2), (2, 64)))
    address_content_matrix = bell_draw(key_list[7], (LAYERS, D, KV_HEADS * 2 * HEAD), D ** -0.5, 0.0625, ((0, 2),))
    projection_back_matrix = bell_draw(key_list[8], (LAYERS, Q_HEADS * HEAD, D), (Q_HEADS * HEAD) ** -0.5, 0.0625, ((0, 2), (1, 64)))
    ending_scale_factors = jnp.clip(1.0 + 0.1 * jax.random.normal(key_list[9], (D,), jnp.float32), 0.5, 1.5).astype(jnp.bfloat16)
    lexicon_matrix = bell_draw(key_list[10], (VOCAB, D), (D // 9) ** -0.5, 0.1875, ((0, 128),))
    sampling_warmth = jnp.clip(jax.random.uniform(key_list[11], (ALL_DECODE_LINES,), jnp.float32, 0.6, 1.4), 0.6, 1.4)
    sampling_noise = draw_sampling_noise(jax.random.fold_in(key_list[13], 71), 0)
    return {"incoming_hidden_states": incoming_hidden_states, "parent_positions": parent_positions, "filled_extents": filled_extents, "stored_address_tensor": stored_address_tensor, "stored_content_tensor": stored_content_tensor, "layer_scale_factors": layer_scale_factors, "question_matrix": question_matrix, "address_content_matrix": address_content_matrix, "projection_back_matrix": projection_back_matrix, "ending_scale_factors": ending_scale_factors, "lexicon_matrix": lexicon_matrix, "sampling_warmth": sampling_warmth, "sampling_noise": sampling_noise}


epsilon = 1e-05

def norm_project(hidden, gain_row, weight):
    hidden_f = hidden.astype(jnp.float32)
    inverse = lax.rsqrt(lax.optimization_barrier(jnp.mean(hidden_f * hidden_f, axis=-1)) + epsilon)
    scaled = (hidden_f * gain_row.astype(jnp.float32)).astype(jnp.bfloat16)
    return jnp.dot(scaled, weight, preferred_element_type=jnp.float32) * inverse[:, None]

def grouped_mixing(question_array, address_content_couple, stored_address_lines, stored_content_lines, extent_each_line):
    row_count = question_array.shape[0]
    slot_count = stored_address_lines.shape[1]
    query_f = question_array.astype(jnp.float32).reshape(row_count, KV_HEADS, -1, HEAD)
    pair_f = address_content_couple.astype(jnp.float32).reshape(row_count, KV_HEADS, 2, HEAD)
    new_key = pair_f[:, :, 0]
    new_value = pair_f[:, :, 1]
    score_scale = HEAD ** (-0.5)
    key_grid = stored_address_lines.reshape(row_count, slot_count, KV_HEADS, HEAD).astype(jnp.float32)
    value_grid = stored_content_lines.reshape(row_count, slot_count, KV_HEADS, HEAD).astype(jnp.float32)
    scores = jnp.einsum('nkgd,nckd->nkgc', query_f, key_grid) * score_scale
    own_score = jnp.einsum('nkgd,nkd->nkg', query_f, new_key) * score_scale
    visible = (jnp.arange(slot_count)[None, :] < extent_each_line[:, None])[:, None, None, :]
    highest = jnp.maximum(lax.optimization_barrier(jnp.max(jnp.where(visible, scores, -1e+30), axis=-1)), own_score)
    weights = jnp.where(visible, jnp.exp(scores - highest[..., None]), 0.0)
    own_weight = jnp.exp(own_score - highest)
    denominator = lax.optimization_barrier(jnp.sum(weights, axis=-1)) + own_weight
    weights_bf = (weights / denominator[..., None]).astype(jnp.bfloat16)
    own_prob = (own_weight / denominator).astype(jnp.bfloat16)
    combined = jnp.einsum('nkgc,nckd->nkgd', weights_bf.astype(jnp.float32), value_grid)
    combined = combined + own_prob.astype(jnp.float32)[..., None] * new_value[:, :, None, :]
    return combined.astype(jnp.bfloat16).reshape(row_count, -1)

def reference(incoming_hidden_states, parent_positions, filled_extents, stored_address_tensor, stored_content_tensor, layer_scale_factors, question_matrix, address_content_matrix, projection_back_matrix, ending_scale_factors, lexicon_matrix, sampling_warmth, sampling_noise):
    extent_each_line = filled_extents[parent_positions]

    def layer_step(hidden, inputs):
        stored_address_lines, stored_content_lines, gain_row, w_query, w_pair, w_output = inputs
        question_array = norm_project(hidden, gain_row, w_query).astype(jnp.bfloat16)
        address_content_couple = norm_project(hidden, gain_row, w_pair).astype(jnp.bfloat16)
        mixed_result = grouped_mixing(question_array, address_content_couple, stored_address_lines[parent_positions], stored_content_lines[parent_positions], extent_each_line)
        combined = hidden.astype(jnp.float32) + jnp.dot(mixed_result, w_output, preferred_element_type=jnp.float32)
        return (combined.astype(jnp.bfloat16), address_content_couple)
    final_rows, new_entries = lax.scan(layer_step, incoming_hidden_states, (stored_address_tensor, stored_content_tensor, layer_scale_factors, question_matrix, address_content_matrix, projection_back_matrix))
    lexicon_scores = norm_project(final_rows, ending_scale_factors, lexicon_matrix.T)
    divided_scores = lexicon_scores / sampling_warmth[:, None]
    top_score = lax.optimization_barrier(jnp.max(divided_scores + sampling_noise, axis=1))
    peak_value = lax.optimization_barrier(jnp.max(divided_scores, axis=1))
    log_norm = peak_value + jnp.log(lax.optimization_barrier(jnp.sum(jnp.exp(divided_scores - peak_value[:, None]), axis=1)))
    return (new_entries, final_rows, top_score, log_norm)
```

```python
import jax
import jax.numpy as jnp
from jax import lax
from jax.sharding import PartitionSpec as P

HEAD = 128
KV_HEADS = 8


epsilon = 1e-05


def scaled_rows(hidden_f, gain_row):
    return (hidden_f * gain_row.astype(jnp.float32)).astype(jnp.bfloat16)


def grouped_mixing(
    queries, new_key, new_value, stored_address_lines, stored_content_lines, extent_each_line
):
    row_count = queries.shape[0]
    slot_count = stored_address_lines.shape[1]
    score_scale = HEAD ** (-0.5)
    scores = (
        jnp.einsum("nd,ncd->nc", queries, stored_address_lines, preferred_element_type=jnp.float32)
        * score_scale
    )
    own_score = (
        jnp.sum(queries.astype(jnp.float32) * new_key.astype(jnp.float32), axis=1) * score_scale
    )
    visible = (
        lax.broadcasted_iota(jnp.int32, (row_count, slot_count), 1) < extent_each_line[:, None]
    )
    highest = jnp.maximum(jnp.max(jnp.where(visible, scores, -1e30), axis=1), own_score)
    weights = jnp.where(visible, jnp.exp(scores - highest[:, None]), 0.0)
    own_weight = jnp.exp(own_score - highest)
    denominator = jnp.sum(weights, axis=1) + own_weight
    weights_bf = (weights / denominator[:, None]).astype(jnp.bfloat16)
    own_prob = (own_weight / denominator).astype(jnp.bfloat16)
    combined = jnp.einsum(
        "nc,ncd->nd", weights_bf, stored_content_lines, preferred_element_type=jnp.float32
    )
    combined = combined + own_prob.astype(jnp.float32)[:, None] * new_value.astype(jnp.float32)
    return combined.astype(jnp.bfloat16)


def per_device(
    incoming_hidden_states,
    parent_positions,
    filled_extents,
    stored_address_tensor,
    stored_content_tensor,
    layer_scale_factors,
    question_matrix,
    address_content_matrix,
    projection_back_matrix,
    ending_scale_factors,
    lexicon_matrix,
    sampling_warmth,
    sampling_noise,
):
    shards = lax.axis_size("tp")
    sections = lax.axis_size("section")
    shard = lax.axis_index("tp")
    section = lax.axis_index("section")
    heads_per_group = shards // KV_HEADS
    group_index = shard // heads_per_group
    pair_width = address_content_matrix.shape[2]
    share_width = pair_width // shards
    share_offset = shard % heads_per_group * share_width
    rows, width = incoming_hidden_states.shape
    chunk = width // shards
    grouped_addresses = lax.dynamic_slice_in_dim(
        stored_address_tensor[0], group_index * HEAD, HEAD, 2
    )
    grouped_contents = lax.dynamic_slice_in_dim(
        stored_content_tensor[0], group_index * HEAD, HEAD, 2
    )
    stored_address_lines = grouped_addresses[parent_positions]
    stored_content_lines = grouped_contents[parent_positions]
    extent_each_line = filled_extents[parent_positions]
    gain_row = layer_scale_factors[0]
    group_pair_weight = lax.dynamic_slice_in_dim(
        address_content_matrix[0], group_index * 2 * HEAD, 2 * HEAD, 1
    )
    w_output = projection_back_matrix[0]

    def layer(hidden):
        hidden_f = hidden.astype(jnp.float32)
        inverse = lax.rsqrt(jnp.mean(hidden_f * hidden_f, axis=1) + epsilon)[:, None]
        scaled = scaled_rows(hidden_f, gain_row)
        queries = jnp.dot(scaled, question_matrix[0], preferred_element_type=jnp.float32) * inverse
        pair = jnp.dot(scaled, group_pair_weight, preferred_element_type=jnp.float32) * inverse
        pair = pair.astype(jnp.bfloat16)
        mixed = grouped_mixing(
            queries.astype(jnp.bfloat16),
            pair[:, :HEAD],
            pair[:, HEAD:],
            stored_address_lines,
            stored_content_lines,
            extent_each_line,
        )
        entry = lax.dynamic_slice_in_dim(pair, share_offset, share_width, 1)
        terms = jnp.dot(mixed, w_output, preferred_element_type=jnp.float32).astype(jnp.bfloat16)
        terms = terms.reshape(rows, shards, chunk).transpose(1, 0, 2)
        terms = lax.all_to_all(terms, "tp", 0, 0)
        summed = jnp.sum(terms.astype(jnp.float32), axis=0)
        own = lax.dynamic_slice_in_dim(hidden, shard * chunk, chunk, 1)
        return (own.astype(jnp.float32) + summed).astype(jnp.bfloat16), entry

    def spread(block, source):
        copies = jnp.broadcast_to(block, (sections * shards, rows, chunk))
        blocks = lax.all_to_all(copies, ("section", "tp"), 0, 0)
        blocks = blocks[source * shards : (source + 1) * shards]
        return blocks.transpose(1, 0, 2).reshape(rows, width)

    block, first_entry = layer(incoming_hidden_states)
    block, entry = layer(spread(block, 0))
    final_rows = spread(block, 1)
    entry = jnp.where(section == 0, first_entry, entry)

    final_f = final_rows.astype(jnp.float32)
    inverse = lax.rsqrt(jnp.mean(final_f * final_f, axis=1) + epsilon)
    lexicon_scores = (
        jnp.einsum(
            "rd,vd->rv",
            scaled_rows(final_f, ending_scale_factors),
            lexicon_matrix,
            preferred_element_type=jnp.float32,
        )
        * inverse[:, None]
    )
    divided_scores = lexicon_scores / sampling_warmth[:, None]
    noisy_best = jnp.max(divided_scores + sampling_noise, axis=1)
    peak_value = jnp.max(divided_scores, axis=1)
    mass_total = jnp.sum(jnp.exp(divided_scores - peak_value[:, None]), axis=1)
    stats = jnp.concatenate([noisy_best, peak_value, mass_total, jnp.zeros((128 - 3 * rows,), jnp.float32)])
    stats = jnp.broadcast_to(stats, (sections * shards, 1, 128))
    stats = lax.all_to_all(stats, ("section", "tp"), 0, 0)[:, 0]
    best_score = jnp.max(stats[:, :rows], axis=0)
    peaks = stats[:, rows : 2 * rows]
    peak_all = jnp.max(peaks, axis=0)
    mass_all = jnp.sum(stats[:, 2 * rows : 3 * rows] * jnp.exp(peaks - peak_all), axis=0)
    log_norm = peak_all + jnp.log(mass_all)
    return (entry[None], final_rows, best_score, log_norm)


def solution(mesh):
    in_specs = (
        P(),
        P(),
        P(),
        P("section", None, None, None),
        P("section", None, None, None),
        P("section", None),
        P("section", None, "tp"),
        P("section", None, None),
        P("section", "tp", None),
        P(),
        P(("section", "tp"), None),
        P(),
        P(None, ("section", "tp")),
    )
    out_specs = (P("section", None, "tp"), P(), P(), P())
    return jax.shard_map(
        per_device, mesh=mesh, in_specs=in_specs, out_specs=out_specs, check_vma=False
    )
```

```python
import functools

import jax
import jax.numpy as jnp
from jax import lax
from jax.experimental import pallas as pl
from jax.experimental.pallas import tpu as pltpu
from jax.sharding import PartitionSpec as P

HEAD = 128
KV_HEADS = 8
STEPS = 4
LIMIT = 24 * 1024 * 1024


epsilon = 1e-05


def dot(a, b, contract=((1,), (0,))):
    return lax.dot_general(a, b, (contract, ((), ())), preferred_element_type=jnp.float32)


def weights_of(width, pieces):
    step = width // pieces
    return [(i * step, step) for i in range(pieces)]


def column_of(scalars, rows):
    row = lax.broadcasted_iota(jnp.int32, (rows, HEAD), 0)
    column = jnp.zeros((rows, HEAD), scalars[0].dtype)
    for j in range(rows):
        column = jnp.where(row == j, scalars[j], column)
    return column


def attend(query, pair, keys, values, visible_slots):
    rows = query.shape[0]
    slots = keys.shape[0] // rows
    new_key = pair[:, :HEAD].astype(jnp.float32)
    new_value = pair[:, HEAD:].astype(jnp.float32)
    score_scale = HEAD ** (-0.5)
    row = lax.broadcasted_iota(jnp.int32, (rows, rows * slots), 0)
    column = lax.broadcasted_iota(jnp.int32, (rows, rows * slots), 1)
    slot = column - row * slots
    visible = (slot >= 0) & (slot < visible_slots[:, :1])
    scores = dot(query, keys, ((1,), (1,))) * score_scale
    own_score = jnp.sum(query.astype(jnp.float32) * new_key, axis=1, keepdims=True) * score_scale
    highest = jnp.maximum(
        jnp.max(jnp.where(visible, scores, -1e30), axis=1, keepdims=True), own_score
    )
    spread = jnp.where(visible, jnp.exp(scores - highest), 0.0)
    own_weight = jnp.exp(own_score - highest)
    denominator = jnp.sum(spread, axis=1, keepdims=True) + own_weight
    probabilities = (spread / denominator).astype(jnp.bfloat16)
    own_prob = (own_weight / denominator).astype(jnp.bfloat16).astype(jnp.float32)
    mixed = dot(probabilities, values) + own_prob * new_value
    return mixed.astype(jnp.bfloat16)


def store_terms(mixed, back, terms_ref, first):
    terms = dot(mixed, back).astype(jnp.bfloat16)
    for k in range(back.shape[1] // HEAD):
        terms_ref[first + k] = terms[:, k * HEAD : (k + 1) * HEAD]


def first_layer_kernel(
    parents_hbm,
    extents_hbm,
    hidden_hbm,
    gain_hbm,
    question_hbm,
    pair_hbm,
    back_hbm,
    address_hbm,
    content_hbm,
    terms_ref,
    entry_ref,
    own_ref,
    gain_ref,
    question_ref,
    pair_ref,
    back_ref,
    keys_ref,
    values_ref,
    visible_ref,
    parents,
    extents,
    hidden_ref,
    address_ref,
    content_ref,
    sems,
    question_sems,
    pair_sems,
    back_sems,
):
    rows, width = hidden_ref.shape
    slots = address_ref.shape[1]
    shard = lax.axis_index("tp")
    group = shard // (lax.axis_size("tp") // KV_HEADS)
    head_columns = pl.ds(pl.multiple_of(group * HEAD, HEAD), HEAD)
    pair_columns = pl.ds(pl.multiple_of(group * 2 * HEAD, 2 * HEAD), 2 * HEAD)
    small = [
        pltpu.make_async_copy(hidden_hbm, hidden_ref, sems.at[0]),
        pltpu.make_async_copy(gain_hbm, gain_ref, sems.at[1]),
        pltpu.make_async_copy(parents_hbm, parents, sems.at[4]),
        pltpu.make_async_copy(extents_hbm, extents, sems.at[5]),
    ]
    lines = [
        pltpu.make_async_copy(address_hbm.at[0, :, :, head_columns], address_ref, sems.at[2]),
        pltpu.make_async_copy(content_hbm.at[0, :, :, head_columns], content_ref, sems.at[3]),
    ]
    projections = []
    for i, (start, step) in enumerate(weights_of(width, STEPS)):
        part = pl.ds(start, step)
        projections.append(
            (
                pltpu.make_async_copy(question_hbm.at[0, part], question_ref.at[part], question_sems.at[i]),
                pltpu.make_async_copy(pair_hbm.at[0, part, pair_columns], pair_ref.at[part], pair_sems.at[i]),
            )
        )
    backs = []
    for i, (start, step) in enumerate(weights_of(width, STEPS)):
        part = pl.ds(start, step)
        backs.append(
            pltpu.make_async_copy(back_hbm.at[0, :, part], back_ref.at[:, part], back_sems.at[i])
        )
    for copy in small:
        copy.start()
    for two in projections:
        for copy in two:
            copy.start()
    for copy in lines:
        copy.start()
    for copy in backs:
        copy.start()

    for copy in small:
        copy.wait()
    own_ref[...] = hidden_ref[:, pl.ds(pl.multiple_of(shard * HEAD, HEAD), HEAD)]
    squares = jnp.zeros((rows, 1), jnp.float32)
    query = jnp.zeros((rows, HEAD), jnp.float32)
    pair = jnp.zeros((rows, 2 * HEAD), jnp.float32)
    for i, (start, step) in enumerate(weights_of(width, STEPS)):
        part = slice(start, start + step)
        hidden = hidden_ref[:, part].astype(jnp.float32)
        squares = squares + jnp.sum(hidden * hidden, axis=1, keepdims=True)
        scaled = (hidden * gain_ref[:, part].astype(jnp.float32)).astype(jnp.bfloat16)
        for copy in projections[i]:
            copy.wait()
        query = query + dot(scaled, question_ref[part])
        pair = pair + dot(scaled, pair_ref[part])
    inverse = lax.rsqrt(squares * (1.0 / width) + epsilon)
    query = (query * inverse).astype(jnp.bfloat16)
    pair = (pair * inverse).astype(jnp.bfloat16)
    entry_ref[...] = pair
    visible = column_of([extents[parents[j]] for j in range(rows)], rows)
    visible_ref[...] = visible
    for copy in lines:
        copy.wait()
    for j in range(rows):
        lines_j = pl.ds(j * slots, slots)
        keys_ref[lines_j] = address_ref[parents[j]]
        values_ref[lines_j] = content_ref[parents[j]]
    mixed = attend(query, pair, keys_ref[...], values_ref[...], visible)
    for i, (start, step) in enumerate(weights_of(width, STEPS)):
        backs[i].wait()
        store_terms(mixed, back_ref[:, start : start + step], terms_ref, start // HEAD)


def next_layer_kernel(
    source,
    blocks_ref,
    first_ref,
    gain_ref,
    question_ref,
    pair_ref,
    back_ref,
    keys_ref,
    values_ref,
    visible_ref,
    ending_hbm,
    lexicon_hbm,
    noise_hbm,
    warmth_hbm,
    terms_ref,
    entry_ref,
    own_ref,
    ending_ref,
    lexicon_ref,
    noise_ref,
    warmth_ref,
    warmth,
    sems,
):
    fetches = [
        pltpu.make_async_copy(warmth_hbm, warmth, sems.at[0]),
        pltpu.make_async_copy(ending_hbm, ending_ref, sems.at[1]),
        pltpu.make_async_copy(noise_hbm, noise_ref, sems.at[2]),
        pltpu.make_async_copy(lexicon_hbm, lexicon_ref, sems.at[3]),
    ]
    for copy in fetches:
        copy.start()
    rows = own_ref.shape[0]
    width = question_ref.shape[0]
    base = source * (width // HEAD)
    shards = lax.axis_size("tp")
    shard = lax.axis_index("tp")
    own_ref[...] = blocks_ref[base + shard]
    squares = jnp.zeros((rows, 1), jnp.float32)
    query = jnp.zeros((rows, HEAD), jnp.float32)
    pair = jnp.zeros((rows, 2 * HEAD), jnp.float32)
    for start, step in weights_of(width, STEPS):
        part = slice(start, start + step)
        hidden = read_blocks(blocks_ref, base + start // HEAD, step // HEAD)
        squares = squares + jnp.sum(hidden * hidden, axis=1, keepdims=True)
        scaled = (hidden * gain_ref[:, part].astype(jnp.float32)).astype(jnp.bfloat16)
        query = query + dot(scaled, question_ref[part])
        pair = pair + dot(scaled, pair_ref[part])
    inverse = lax.rsqrt(squares * (1.0 / width) + epsilon)
    query = (query * inverse).astype(jnp.bfloat16)
    pair = (pair * inverse).astype(jnp.bfloat16)
    both = jnp.where(lax.axis_index("section") == 0, first_ref[...], pair).astype(jnp.float32)
    share = entry_ref.shape[1]
    offset = shard % (shards // KV_HEADS) * share
    both = pltpu.roll(both, 2 * HEAD - offset, 1)
    entry_ref[...] = both[:, :share].astype(jnp.bfloat16)
    mixed = attend(query, pair, keys_ref[...], values_ref[...], visible_ref[...])
    for start, step in weights_of(width, STEPS):
        store_terms(mixed, back_ref[:, start : start + step], terms_ref, start // HEAD)
    for copy in fetches:
        copy.wait()
    warmth_ref[...] = column_of([warmth[j] for j in range(rows)], rows)


def read_blocks(blocks_ref, first, count):
    return jnp.concatenate([blocks_ref[first + k] for k in range(count)], axis=1).astype(jnp.float32)


def in_hbm(*arrays):
    return [pltpu.with_memory_space_constraint(a, pltpu.HBM) for a in arrays]


def specs(kinds):
    spaces = {"s": pltpu.SMEM, "v": pltpu.VMEM, "h": pltpu.HBM}
    return [pl.BlockSpec(memory_space=spaces[kind]) for kind in kinds]


def first_layer(parents, extents, hidden, gain, question, pair, back, address, content):
    rows, width = hidden.shape
    slots = address.shape[2]
    bf16 = functools.partial(jax.ShapeDtypeStruct, dtype=jnp.bfloat16)
    return pl.pallas_call(
        first_layer_kernel,
        out_shape=(
            bf16((width // HEAD, rows, HEAD)),
            bf16((rows, 2 * HEAD)),
            bf16((rows, HEAD)),
            bf16((1, width)),
            bf16((width, HEAD)),
            bf16((width, 2 * HEAD)),
            bf16((HEAD, width)),
            bf16((rows * slots, HEAD)),
            bf16((rows * slots, HEAD)),
            jax.ShapeDtypeStruct((rows, HEAD), jnp.int32),
        ),
        in_specs=specs("hhhhhhhhh"),
        out_specs=specs("v" * 10),
        scratch_shapes=[
            pltpu.SMEM((rows,), jnp.int32),
            pltpu.SMEM((rows,), jnp.int32),
            pltpu.VMEM((rows, width), jnp.bfloat16),
            pltpu.VMEM((rows, slots, HEAD), jnp.bfloat16),
            pltpu.VMEM((rows, slots, HEAD), jnp.bfloat16),
            pltpu.SemaphoreType.DMA((6,)),
            pltpu.SemaphoreType.DMA((STEPS,)),
            pltpu.SemaphoreType.DMA((STEPS,)),
            pltpu.SemaphoreType.DMA((STEPS,)),
        ],
        compiler_params=pltpu.CompilerParams(vmem_limit_bytes=LIMIT),
        name="first_layer",
    )(*in_hbm(parents, extents, hidden, gain, question, pair, back, address, content))


def next_layer(source, blocks, first, held, ending, lexicon, noise, warmth, share):
    rows = warmth.shape[0]
    width = lexicon.shape[1]
    bf16 = functools.partial(jax.ShapeDtypeStruct, dtype=jnp.bfloat16)
    return pl.pallas_call(
        functools.partial(next_layer_kernel, source),
        out_shape=(
            bf16((width // HEAD, rows, HEAD)),
            bf16((rows, share)),
            bf16((rows, HEAD)),
            bf16(ending.shape),
            bf16(lexicon.shape),
            jax.ShapeDtypeStruct(noise.shape, jnp.float32),
            jax.ShapeDtypeStruct((rows, HEAD), jnp.float32),
        ),
        in_specs=specs("v" * (2 + len(held)) + "hhhh"),
        out_specs=specs("v" * 7),
        scratch_shapes=[pltpu.SMEM((rows,), jnp.float32), pltpu.SemaphoreType.DMA((4,))],
        compiler_params=pltpu.CompilerParams(vmem_limit_bytes=LIMIT),
        name="next_layer",
    )(blocks, first, *held, *in_hbm(ending, lexicon, noise, warmth))


def stats_kernel(source, blocks_ref, gain_ref, warmth_ref, noise_ref, lexicon_ref, out_ref, final_ref):
    rows, width = final_ref.shape
    base = source * (width // HEAD)
    squares = jnp.zeros((rows, HEAD), jnp.float32)
    logits = jnp.zeros((rows, lexicon_ref.shape[0]), jnp.float32)
    for start, step in weights_of(width, STEPS):
        part = slice(start, start + step)
        pieces = []
        for k in range(start // HEAD, (start + step) // HEAD):
            block = blocks_ref[base + k]
            final_ref[:, k * HEAD : (k + 1) * HEAD] = block
            hidden = block.astype(jnp.float32)
            squares = squares + hidden * hidden
            pieces.append((hidden * gain_ref[k : k + 1].astype(jnp.float32)).astype(jnp.bfloat16))
        scaled = jnp.concatenate(pieces, axis=1)
        logits = logits + dot(scaled, lexicon_ref[:, part], ((1,), (1,)))
    squares = jnp.sum(squares, axis=1, keepdims=True)
    inverse = lax.rsqrt(squares * (1.0 / width) + epsilon)
    tempered = logits * inverse / warmth_ref[:, :1]
    best = jnp.max(tempered + noise_ref[...], axis=1, keepdims=True)
    peak = jnp.max(tempered, axis=1, keepdims=True)
    mass = jnp.sum(jnp.exp(tempered - peak), axis=1, keepdims=True)
    norm = peak + jnp.log(mass)
    lane = lax.broadcasted_iota(jnp.int32, (rows, HEAD), 1)
    row = lax.broadcasted_iota(jnp.int32, (rows, HEAD), 0)
    packed = jnp.where(lane == row, best, 0.0)
    packed = jnp.where(lane == row + rows, norm, packed)
    packed = jnp.sum(packed, axis=0, keepdims=True)
    out_ref[...] = jnp.broadcast_to(packed[None], out_ref.shape)


def local_stats(source, blocks, gain, warmth, noise, lexicon):
    rows = warmth.shape[0]
    width = lexicon.shape[1]
    return pl.pallas_call(
        functools.partial(stats_kernel, source),
        out_shape=(
            jax.ShapeDtypeStruct((blocks.shape[0], 1, HEAD), jnp.float32),
            jax.ShapeDtypeStruct((rows, width), jnp.bfloat16),
        ),
        in_specs=specs("vvvvv"),
        out_specs=tuple(specs("vv")),
        compiler_params=pltpu.CompilerParams(vmem_limit_bytes=LIMIT),
        name="local_stats",
    )(blocks, gain, warmth, noise, lexicon)


def combine_kernel(stats_ref, best_ref, norm_ref):
    rows = best_ref.shape[0]
    stats = stats_ref[...]
    highest = jnp.max(stats, axis=0)
    norm = highest + jnp.log(jnp.sum(jnp.exp(stats - highest[None]), axis=0))
    best_ref[...] = highest[0, :rows]
    norm_ref[...] = norm[0, rows : 2 * rows]


def combine(stats, rows):
    row = jax.ShapeDtypeStruct((rows,), jnp.float32)
    return pl.pallas_call(
        combine_kernel,
        out_shape=(row, row),
        in_specs=specs("v"),
        out_specs=specs("vv"),
        name="combine",
    )(stats)


def per_device(
    incoming_hidden_states,
    parent_positions,
    filled_extents,
    stored_address_tensor,
    stored_content_tensor,
    layer_scale_factors,
    question_matrix,
    address_content_matrix,
    projection_back_matrix,
    ending_scale_factors,
    lexicon_matrix,
    sampling_warmth,
    sampling_noise,
):
    shards = lax.axis_size("tp")
    sections = lax.axis_size("section")
    rows, width = incoming_hidden_states.shape
    chunk = width // shards
    share = address_content_matrix.shape[2] // shards

    def exchange(terms, own):
        terms = lax.all_to_all(terms, "tp", 0, 0)
        summed = jnp.sum(terms.astype(jnp.float32), axis=0)
        block = (own.astype(jnp.float32) + summed).astype(jnp.bfloat16)
        copies = jnp.broadcast_to(block, (sections * shards, rows, chunk))
        return lax.all_to_all(copies, ("section", "tp"), 0, 0)

    terms, first, own, *held = first_layer(
        parent_positions,
        filled_extents,
        incoming_hidden_states,
        layer_scale_factors,
        question_matrix,
        address_content_matrix,
        projection_back_matrix,
        stored_address_tensor,
        stored_content_tensor,
    )
    blocks = exchange(terms, own)
    terms, entry, own, gain, lexicon, noise, warmth = next_layer(
        0,
        blocks,
        first,
        held,
        ending_scale_factors.reshape(width // HEAD, HEAD),
        lexicon_matrix,
        sampling_noise,
        sampling_warmth,
        share,
    )
    blocks = exchange(terms, own)
    stats, final_rows = local_stats(1, blocks, gain, warmth, noise, lexicon)
    stats = lax.all_to_all(stats, ("section", "tp"), 0, 0)
    best_score, log_norm = combine(stats, rows)
    return (entry[None], final_rows, best_score, log_norm)


def solution(mesh):
    in_specs = (
        P(),
        P(),
        P(),
        P("section", None, None, None),
        P("section", None, None, None),
        P("section", None),
        P("section", None, "tp"),
        P("section", None, None),
        P("section", "tp", None),
        P(),
        P(("section", "tp"), None),
        P(),
        P(None, ("section", "tp")),
    )
    out_specs = (P("section", None, "tp"), P(), P(), P())
    return jax.shard_map(
        per_device, mesh=mesh, in_specs=in_specs, out_specs=out_specs, check_vma=False
    )
```

```python
import functools

import jax
import jax.numpy as jnp
from jax import lax
from jax.experimental import pallas as pl
from jax.experimental.pallas import tpu as pltpu
from jax.sharding import PartitionSpec as P

HEAD = 128
KV_HEADS = 8
STEPS = 4
LIMIT = 16 * 1024 * 1024


epsilon = 1e-05


def dot(a, b, contract=((1,), (0,))):
    return lax.dot_general(a, b, (contract, ((), ())), preferred_element_type=jnp.float32)


def weights_of(width, pieces):
    step = width // pieces
    return [(i * step, step) for i in range(pieces)]


def column_of(scalars, rows):
    row = lax.broadcasted_iota(jnp.int32, (rows, HEAD), 0)
    column = jnp.zeros((rows, HEAD), scalars[0].dtype)
    for j in range(rows):
        column = jnp.where(row == j, scalars[j], column)
    return column


def attend(query, pair, keys, values, visible_slots):
    rows = query.shape[0]
    slots = keys.shape[0] // rows
    new_key = pair[:, :HEAD].astype(jnp.float32)
    new_value = pair[:, HEAD:].astype(jnp.float32)
    score_scale = HEAD ** (-0.5)
    row = lax.broadcasted_iota(jnp.int32, (rows, rows * slots), 0)
    column = lax.broadcasted_iota(jnp.int32, (rows, rows * slots), 1)
    slot = column - row * slots
    visible = (slot >= 0) & (slot < visible_slots[:, :1])
    scores = dot(query, keys, ((1,), (1,))) * score_scale
    own_score = jnp.sum(query.astype(jnp.float32) * new_key, axis=1, keepdims=True) * score_scale
    highest = jnp.maximum(
        jnp.max(jnp.where(visible, scores, -1e30), axis=1, keepdims=True), own_score
    )
    spread = jnp.where(visible, jnp.exp(scores - highest), 0.0)
    own_weight = jnp.exp(own_score - highest)
    denominator = jnp.sum(spread, axis=1, keepdims=True) + own_weight
    probabilities = (spread / denominator).astype(jnp.bfloat16)
    own_prob = (own_weight / denominator).astype(jnp.bfloat16).astype(jnp.float32)
    mixed = dot(probabilities, values) + own_prob * new_value
    return mixed.astype(jnp.bfloat16)


def store_terms(mixed, back, terms_ref):
    terms = dot(mixed, back)
    rows = terms_ref.shape[1]
    parts = mixed.shape[0] // rows
    shards = terms_ref.shape[0] // parts
    for k in range(back.shape[1] // HEAD):
        for p in range(parts):
            block = terms[p * rows : (p + 1) * rows, k * HEAD : (k + 1) * HEAD]
            terms_ref[p * shards + k] = block.astype(jnp.bfloat16)


def lane_squares(hidden):
    total = hidden[:, :HEAD] * hidden[:, :HEAD]
    for k in range(HEAD, hidden.shape[1], HEAD):
        total = total + hidden[:, k : k + HEAD] * hidden[:, k : k + HEAD]
    return total


def share_of(block, own_ref):
    rows = own_ref.shape[0]
    own = block[:rows]
    for p in range(1, block.shape[0] // rows):
        own = jnp.where(lax.axis_index("section") == p, block[p * rows : (p + 1) * rows], own)
    own_ref[...] = own


def whole_rows(blocks_ref, shards, k):
    parts = [blocks_ref[i + k].astype(jnp.float32) for i in range(0, blocks_ref.shape[0], shards)]
    return jnp.concatenate(parts, axis=0)


def first_layer_kernel(
    parents_hbm,
    extents_hbm,
    hidden_hbm,
    gain_hbm,
    question_hbm,
    pair_hbm,
    back_hbm,
    address_hbm,
    content_hbm,
    terms_ref,
    entry_ref,
    own_ref,
    gain_ref,
    question_ref,
    pair_ref,
    back_ref,
    keys_ref,
    values_ref,
    visible_ref,
    parents,
    extents,
    hidden_ref,
    address_ref,
    content_ref,
    sems,
    question_sems,
    pair_sems,
):
    rows, width = hidden_ref.shape
    slots = address_ref.shape[1]
    shard = lax.axis_index("tp")
    group = shard // (lax.axis_size("tp") // KV_HEADS)
    head_columns = pl.ds(pl.multiple_of(group * HEAD, HEAD), HEAD)
    pair_columns = pl.ds(pl.multiple_of(group * 2 * HEAD, 2 * HEAD), 2 * HEAD)
    small = [
        pltpu.make_async_copy(hidden_hbm, hidden_ref, sems.at[0]),
        pltpu.make_async_copy(gain_hbm, gain_ref, sems.at[1]),
        pltpu.make_async_copy(parents_hbm, parents, sems.at[4]),
        pltpu.make_async_copy(extents_hbm, extents, sems.at[5]),
    ]
    lines = [
        pltpu.make_async_copy(address_hbm.at[0, :, :, head_columns], address_ref, sems.at[2]),
        pltpu.make_async_copy(content_hbm.at[0, :, :, head_columns], content_ref, sems.at[3]),
    ]
    projections = []
    for i, (start, step) in enumerate(weights_of(width, STEPS)):
        part = pl.ds(start, step)
        projections.append(
            (
                pltpu.make_async_copy(question_hbm.at[0, part], question_ref.at[part], question_sems.at[i]),
                pltpu.make_async_copy(pair_hbm.at[0, part, pair_columns], pair_ref.at[part], pair_sems.at[i]),
            )
        )
    back = pltpu.make_async_copy(back_hbm.at[0], back_ref, sems.at[6])
    for copy in small:
        copy.start()
    for i, two in enumerate(projections):
        for copy in two:
            copy.start()
        if i == 0:
            for copy in lines:
                copy.start()
    back.start()

    for copy in small:
        copy.wait()
    own = hidden_ref[:, pl.ds(pl.multiple_of(shard * HEAD, HEAD), HEAD)]
    share_of(own.astype(jnp.float32), own_ref)
    squares = jnp.zeros((rows, HEAD), jnp.float32)
    query = jnp.zeros((rows, HEAD), jnp.float32)
    pair = jnp.zeros((rows, 2 * HEAD), jnp.float32)
    for i, (start, step) in enumerate(weights_of(width, STEPS)):
        part = slice(start, start + step)
        hidden = hidden_ref[:, part].astype(jnp.float32)
        squares = squares + lane_squares(hidden)
        scaled = (hidden * gain_ref[:, part].astype(jnp.float32)).astype(jnp.bfloat16)
        if i == STEPS // 2:
            visible = column_of([extents[parents[j]] for j in range(rows)], rows)
            visible_ref[...] = visible
            for copy in lines:
                copy.wait()
            for j in range(rows):
                lines_j = pl.ds(j * slots, slots)
                keys_ref[lines_j] = address_ref[parents[j]]
                values_ref[lines_j] = content_ref[parents[j]]
        for copy in projections[i]:
            copy.wait()
        query = query + dot(scaled, question_ref[part])
        pair = pair + dot(scaled, pair_ref[part])
    squares = jnp.sum(squares, axis=1, keepdims=True)
    inverse = lax.rsqrt(squares * (1.0 / width) + epsilon)
    query = (query * inverse).astype(jnp.bfloat16)
    pair = (pair * inverse).astype(jnp.bfloat16)
    entry_ref[...] = pair
    mixed = attend(query, pair, keys_ref[...], values_ref[...], visible)
    back.wait()
    store_terms(mixed, back_ref[...], terms_ref)


def next_layer_kernel(
    blocks_ref,
    first_ref,
    gain_ref,
    question_ref,
    pair_ref,
    back_ref,
    keys_ref,
    values_ref,
    visible_ref,
    warmth_hbm,
    terms_ref,
    entry_hbm,
    own_ref,
    warmth_ref,
    entry_ref,
    warmth,
    sems,
):
    fetch = pltpu.make_async_copy(warmth_hbm, warmth, sems.at[0])
    fetch.start()
    width = question_ref.shape[0]
    shards = lax.axis_size("tp")
    shard = lax.axis_index("tp")
    rows = first_ref.shape[0]
    share_of(whole_rows(blocks_ref, shards, shard), own_ref)
    hidden = jnp.concatenate([whole_rows(blocks_ref, shards, k) for k in range(shards)], axis=1)
    squares = lane_squares(hidden)
    scaled = (hidden * gain_ref[...].astype(jnp.float32)).astype(jnp.bfloat16)
    query = dot(scaled, question_ref[...])
    pair = dot(scaled, pair_ref[...])
    squares = jnp.sum(squares, axis=1, keepdims=True)
    inverse = lax.rsqrt(squares * (1.0 / width) + epsilon)
    query = (query * inverse).astype(jnp.bfloat16)
    pair = (pair * inverse).astype(jnp.bfloat16)
    both = jnp.where(lax.axis_index("section") == 0, first_ref[...], pair).astype(jnp.float32)
    share = entry_ref.shape[1]
    offset = shard % (shards // KV_HEADS) * share
    both = pltpu.roll(both, 2 * HEAD - offset, 1)
    entry_ref[...] = both[:, :share].astype(jnp.bfloat16)
    leave = pltpu.make_async_copy(entry_ref, entry_hbm, sems.at[1])
    leave.start()
    fetch.wait()
    warmth_ref[...] = column_of([warmth[j] for j in range(rows)], rows)
    mixed = attend(query, pair, keys_ref[...], values_ref[...], visible_ref[...])
    store_terms(mixed, back_ref[...], terms_ref)
    leave.wait()


def in_hbm(*arrays):
    return [pltpu.with_memory_space_constraint(a, pltpu.HBM) for a in arrays]


def specs(kinds):
    spaces = {"s": pltpu.SMEM, "v": pltpu.VMEM, "h": pltpu.HBM}
    return [pl.BlockSpec(memory_space=spaces[kind]) for kind in kinds]


def first_layer(terms_shape, parents, extents, hidden, gain, question, pair, back, address, content):
    rows, width = hidden.shape
    slots = address.shape[2]
    bf16 = functools.partial(jax.ShapeDtypeStruct, dtype=jnp.bfloat16)
    return pl.pallas_call(
        first_layer_kernel,
        out_shape=(
            bf16(terms_shape),
            bf16((rows, 2 * HEAD)),
            jax.ShapeDtypeStruct(terms_shape[1:], jnp.float32),
            bf16((1, width)),
            bf16((width, HEAD)),
            bf16((width, 2 * HEAD)),
            bf16((HEAD, width)),
            bf16((rows * slots, HEAD)),
            bf16((rows * slots, HEAD)),
            jax.ShapeDtypeStruct((rows, HEAD), jnp.int32),
        ),
        in_specs=specs("hhhhhhhhh"),
        out_specs=specs("v" * 10),
        scratch_shapes=[
            pltpu.SMEM((rows,), jnp.int32),
            pltpu.SMEM((rows,), jnp.int32),
            pltpu.VMEM((rows, width), jnp.bfloat16),
            pltpu.VMEM((rows, slots, HEAD), jnp.bfloat16),
            pltpu.VMEM((rows, slots, HEAD), jnp.bfloat16),
            pltpu.SemaphoreType.DMA((7,)),
            pltpu.SemaphoreType.DMA((STEPS,)),
            pltpu.SemaphoreType.DMA((STEPS,)),
        ],
        compiler_params=pltpu.CompilerParams(vmem_limit_bytes=LIMIT),
        name="first_layer",
    )(*in_hbm(parents, extents, hidden, gain, question, pair, back, address, content))


def next_layer(blocks, first, held, warmth, share):
    rows = warmth.shape[0]
    bf16 = functools.partial(jax.ShapeDtypeStruct, dtype=jnp.bfloat16)
    return pl.pallas_call(
        next_layer_kernel,
        out_shape=(
            bf16(blocks.shape),
            bf16((rows, share)),
            jax.ShapeDtypeStruct(blocks.shape[1:], jnp.float32),
            jax.ShapeDtypeStruct((rows, HEAD), jnp.float32),
        ),
        in_specs=specs("v" * (2 + len(held)) + "h"),
        out_specs=specs("vhvv"),
        scratch_shapes=[
            pltpu.VMEM((rows, share), jnp.bfloat16),
            pltpu.SMEM((rows,), jnp.float32),
            pltpu.SemaphoreType.DMA((2,)),
        ],
        compiler_params=pltpu.CompilerParams(vmem_limit_bytes=LIMIT),
        name="next_layer",
    )(blocks, first, *held, *in_hbm(warmth))


def stats_kernel(
    blocks_ref, gain_ref, warmth_ref, noise_ref, lexicon_ref, out_ref, final_hbm, final_ref, sem
):
    rows, width = final_ref.shape
    shards = width // HEAD
    squares = jnp.zeros((rows, HEAD), jnp.float32)
    pieces = []
    for k in range(shards):
        hidden = whole_rows(blocks_ref, shards, k)
        final_ref[:, k * HEAD : (k + 1) * HEAD] = hidden.astype(jnp.bfloat16)
        squares = squares + hidden * hidden
        pieces.append((hidden * gain_ref[k : k + 1].astype(jnp.float32)).astype(jnp.bfloat16))
    leave = pltpu.make_async_copy(final_ref, final_hbm, sem)
    leave.start()
    logits = dot(jnp.concatenate(pieces, axis=1), lexicon_ref[...], ((1,), (1,)))
    squares = jnp.sum(squares, axis=1, keepdims=True)
    inverse = lax.rsqrt(squares * (1.0 / width) + epsilon)
    tempered = logits * inverse / warmth_ref[:, :1]
    best = jnp.max(tempered + noise_ref[...], axis=1, keepdims=True)
    peak = jnp.max(tempered, axis=1, keepdims=True)
    mass = jnp.sum(jnp.exp(tempered - peak), axis=1, keepdims=True)
    norm = peak + jnp.log(mass)
    lane = lax.broadcasted_iota(jnp.int32, (rows, HEAD), 1)
    row = lax.broadcasted_iota(jnp.int32, (rows, HEAD), 0)
    packed = jnp.where(lane == row, best, 0.0)
    packed = jnp.where(lane == row + rows, norm, packed)
    packed = jnp.sum(packed, axis=0, keepdims=True)
    out_ref[...] = jnp.broadcast_to(packed[None], out_ref.shape)
    leave.wait()


def local_stats(blocks, gain, warmth, noise, lexicon):
    rows = warmth.shape[0]
    width = lexicon.shape[1]
    return pl.pallas_call(
        stats_kernel,
        out_shape=(
            jax.ShapeDtypeStruct((blocks.shape[0], 1, HEAD), jnp.float32),
            jax.ShapeDtypeStruct((rows, width), jnp.bfloat16),
        ),
        in_specs=specs("vvvvv"),
        out_specs=tuple(specs("vh")),
        scratch_shapes=[pltpu.VMEM((rows, width), jnp.bfloat16), pltpu.SemaphoreType.DMA],
        compiler_params=pltpu.CompilerParams(vmem_limit_bytes=LIMIT),
        name="local_stats",
    )(blocks, gain, warmth, noise, lexicon)


def combine_kernel(stats_ref, best_hbm, norm_hbm, best_ref, norm_ref, sems):
    rows = best_ref.shape[0]
    stats = stats_ref[...]
    highest = jnp.max(stats, axis=0)
    norm = highest + jnp.log(jnp.sum(jnp.exp(stats - highest[None]), axis=0))
    best_ref[...] = highest[0, :rows]
    norm_ref[...] = norm[0, rows : 2 * rows]
    copies = [
        pltpu.make_async_copy(best_ref, best_hbm, sems.at[0]),
        pltpu.make_async_copy(norm_ref, norm_hbm, sems.at[1]),
    ]
    for copy in copies:
        copy.start()
    for copy in copies:
        copy.wait()


def combine(stats, rows):
    row = jax.ShapeDtypeStruct((rows,), jnp.float32)
    return pl.pallas_call(
        combine_kernel,
        out_shape=(row, row),
        in_specs=specs("v"),
        out_specs=specs("hh"),
        compiler_params=pltpu.CompilerParams(vmem_limit_bytes=LIMIT // 4),
        scratch_shapes=[
            pltpu.VMEM((rows,), jnp.float32),
            pltpu.VMEM((rows,), jnp.float32),
            pltpu.SemaphoreType.DMA((2,)),
        ],
        name="combine",
    )(stats)


def per_device(
    incoming_hidden_states,
    parent_positions,
    filled_extents,
    stored_address_tensor,
    stored_content_tensor,
    layer_scale_factors,
    question_matrix,
    address_content_matrix,
    projection_back_matrix,
    ending_scale_factors,
    lexicon_matrix,
    sampling_warmth,
    sampling_noise,
):
    shards = lax.axis_size("tp")
    sections = lax.axis_size("section")
    rows, width = incoming_hidden_states.shape
    share = address_content_matrix.shape[2] // shards
    terms_shape = (sections * shards, rows // sections, width // shards)

    def exchange(terms, own, source):
        terms = lax.all_to_all(terms, ("section", "tp"), 0, 0)
        terms = terms[source * shards : (source + 1) * shards]
        block = (own + jnp.sum(terms.astype(jnp.float32), axis=0)).astype(jnp.bfloat16)
        copies = jnp.broadcast_to(block, terms_shape)
        return lax.all_to_all(copies, ("section", "tp"), 0, 0)

    terms, first, own, *held = first_layer(
        terms_shape,
        parent_positions,
        filled_extents,
        incoming_hidden_states,
        layer_scale_factors,
        question_matrix,
        address_content_matrix,
        projection_back_matrix,
        stored_address_tensor,
        stored_content_tensor,
    )
    blocks = exchange(terms, own, 0)
    terms, entry, own, warmth = next_layer(
        blocks,
        first,
        held,
        sampling_warmth,
        share,
    )
    blocks = exchange(terms, own, 1)
    stats, final_rows = local_stats(
        blocks,
        ending_scale_factors.reshape(width // HEAD, HEAD),
        warmth,
        sampling_noise,
        lexicon_matrix,
    )
    stats = lax.all_to_all(stats, ("section", "tp"), 0, 0)
    best_score, log_norm = combine(stats, rows)
    return (entry[None], final_rows, best_score, log_norm)


def solution(mesh):
    in_specs = (
        P(),
        P(),
        P(),
        P("section", None, None, None),
        P("section", None, None, None),
        P("section", None),
        P("section", None, "tp"),
        P("section", None, None),
        P("section", "tp", None),
        P(),
        P(("section", "tp"), None),
        P(),
        P(None, ("section", "tp")),
    )
    out_specs = (P("section", None, "tp"), P(), P(), P())
    return jax.shard_map(
        per_device, mesh=mesh, in_specs=in_specs, out_specs=out_specs, check_vma=False
    )
```

```python
import functools

import jax
import jax.numpy as jnp
from jax import lax
from jax.experimental import pallas as pl
from jax.experimental.pallas import tpu as pltpu
from jax.sharding import PartitionSpec as P

HEAD = 128
KV_HEADS = 8
STEPS = 4
LIMIT = 16 * 1024 * 1024


epsilon = 1e-05


def dot(a, b, contract=((1,), (0,))):
    return lax.dot_general(a, b, (contract, ((), ())), preferred_element_type=jnp.float32)


def weights_of(width, pieces):
    step = width // pieces
    return [(i * step, step) for i in range(pieces)]


def column_of(scalars, rows):
    row = lax.broadcasted_iota(jnp.int32, (rows, HEAD), 0)
    column = jnp.zeros((rows, HEAD), scalars[0].dtype)
    for j in range(rows):
        column = jnp.where(row == j, scalars[j], column)
    return column


def attend(query, pair, keys, values, visible_slots):
    rows = query.shape[0]
    slots = keys.shape[0] // rows
    new_key = pair[:, :HEAD].astype(jnp.float32)
    new_value = pair[:, HEAD:].astype(jnp.float32)
    score_scale = HEAD ** (-0.5)
    row = lax.broadcasted_iota(jnp.int32, (rows, rows * slots), 0)
    column = lax.broadcasted_iota(jnp.int32, (rows, rows * slots), 1)
    slot = column - row * slots
    visible = (slot >= 0) & (slot < visible_slots[:, :1])
    scores = dot(query, keys, ((1,), (1,))) * score_scale
    own_score = jnp.sum(query.astype(jnp.float32) * new_key, axis=1, keepdims=True) * score_scale
    highest = jnp.maximum(
        jnp.max(jnp.where(visible, scores, -1e30), axis=1, keepdims=True), own_score
    )
    spread = jnp.where(visible, jnp.exp(scores - highest), 0.0)
    own_weight = jnp.exp(own_score - highest)
    denominator = jnp.sum(spread, axis=1, keepdims=True) + own_weight
    probabilities = (spread / denominator).astype(jnp.bfloat16)
    own_prob = (own_weight / denominator).astype(jnp.bfloat16).astype(jnp.float32)
    mixed = dot(probabilities, values) + own_prob * new_value
    return mixed.astype(jnp.bfloat16)


def store_terms(mixed, back, terms_ref):
    terms = dot(mixed, back)
    rows = terms_ref.shape[1]
    parts = mixed.shape[0] // rows
    shards = terms_ref.shape[0] // parts
    for k in range(back.shape[1] // HEAD):
        for p in range(parts):
            block = terms[p * rows : (p + 1) * rows, k * HEAD : (k + 1) * HEAD]
            terms_ref[p * shards + k] = block.astype(jnp.bfloat16)


def lane_squares(hidden):
    total = hidden[:, :HEAD] * hidden[:, :HEAD]
    for k in range(HEAD, hidden.shape[1], HEAD):
        total = total + hidden[:, k : k + HEAD] * hidden[:, k : k + HEAD]
    return total


def share_of(block, own_ref):
    rows = own_ref.shape[0]
    own = block[:rows]
    for p in range(1, block.shape[0] // rows):
        own = jnp.where(lax.axis_index("section") == p, block[p * rows : (p + 1) * rows], own)
    own_ref[...] = own


def whole_rows(blocks_ref, shards, k):
    parts = [blocks_ref[i + k].astype(jnp.float32) for i in range(0, blocks_ref.shape[0], shards)]
    return jnp.concatenate(parts, axis=0)


def first_layer_kernel(
    parents_hbm,
    extents_hbm,
    warmth_hbm,
    hidden_hbm,
    gain_hbm,
    question_hbm,
    pair_hbm,
    back_hbm,
    address_hbm,
    content_hbm,
    terms_ref,
    entry_ref,
    own_ref,
    gain_ref,
    question_ref,
    pair_ref,
    back_ref,
    keys_ref,
    values_ref,
    visible_ref,
    warmth_ref,
    parents,
    extents,
    warmth,
    hidden_ref,
    address_ref,
    content_ref,
    sems,
    question_sems,
    pair_sems,
):
    rows, width = hidden_ref.shape
    slots = address_ref.shape[1]
    shard = lax.axis_index("tp")
    group = shard // (lax.axis_size("tp") // KV_HEADS)
    head_columns = pl.ds(pl.multiple_of(group * HEAD, HEAD), HEAD)
    pair_columns = pl.ds(pl.multiple_of(group * 2 * HEAD, 2 * HEAD), 2 * HEAD)
    small = [
        pltpu.make_async_copy(hidden_hbm, hidden_ref, sems.at[0]),
        pltpu.make_async_copy(gain_hbm, gain_ref, sems.at[1]),
        pltpu.make_async_copy(parents_hbm, parents, sems.at[4]),
        pltpu.make_async_copy(extents_hbm, extents, sems.at[5]),
        pltpu.make_async_copy(warmth_hbm, warmth, sems.at[7]),
    ]
    lines = [
        pltpu.make_async_copy(address_hbm.at[0, :, :, head_columns], address_ref, sems.at[2]),
        pltpu.make_async_copy(content_hbm.at[0, :, :, head_columns], content_ref, sems.at[3]),
    ]
    projections = []
    for i, (start, step) in enumerate(weights_of(width, STEPS)):
        part = pl.ds(start, step)
        projections.append(
            (
                pltpu.make_async_copy(question_hbm.at[0, part], question_ref.at[part], question_sems.at[i]),
                pltpu.make_async_copy(pair_hbm.at[0, part, pair_columns], pair_ref.at[part], pair_sems.at[i]),
            )
        )
    back = pltpu.make_async_copy(back_hbm.at[0], back_ref, sems.at[6])
    for copy in small:
        copy.start()
    for i, two in enumerate(projections):
        for copy in two:
            copy.start()
        if i == 0:
            for copy in lines:
                copy.start()
    back.start()

    for copy in small:
        copy.wait()
    own = hidden_ref[:, pl.ds(pl.multiple_of(shard * HEAD, HEAD), HEAD)]
    share_of(own.astype(jnp.float32), own_ref)
    squares = jnp.zeros((rows, HEAD), jnp.float32)
    query = jnp.zeros((rows, HEAD), jnp.float32)
    pair = jnp.zeros((rows, 2 * HEAD), jnp.float32)
    for i, (start, step) in enumerate(weights_of(width, STEPS)):
        part = slice(start, start + step)
        hidden = hidden_ref[:, part].astype(jnp.float32)
        squares = squares + lane_squares(hidden)
        scaled = (hidden * gain_ref[:, part].astype(jnp.float32)).astype(jnp.bfloat16)
        if i == STEPS // 2:
            visible = column_of([extents[parents[j]] for j in range(rows)], rows)
            visible_ref[...] = visible
            warmth_ref[...] = column_of([warmth[j] for j in range(rows)], rows)
            for copy in lines:
                copy.wait()
            for j in range(rows):
                lines_j = pl.ds(j * slots, slots)
                keys_ref[lines_j] = address_ref[parents[j]]
                values_ref[lines_j] = content_ref[parents[j]]
        for copy in projections[i]:
            copy.wait()
        query = query + dot(scaled, question_ref[part])
        pair = pair + dot(scaled, pair_ref[part])
    squares = jnp.sum(squares, axis=1, keepdims=True)
    inverse = lax.rsqrt(squares * (1.0 / width) + epsilon)
    query = (query * inverse).astype(jnp.bfloat16)
    pair = (pair * inverse).astype(jnp.bfloat16)
    entry_ref[...] = pair
    mixed = attend(query, pair, keys_ref[...], values_ref[...], visible)
    back.wait()
    store_terms(mixed, back_ref[...], terms_ref)


def next_layer_kernel(
    blocks_ref,
    first_ref,
    gain_ref,
    question_ref,
    pair_ref,
    back_ref,
    keys_ref,
    values_ref,
    visible_ref,
    terms_ref,
    entry_hbm,
    own_ref,
    entry_ref,
    sem,
):
    width = question_ref.shape[0]
    shards = lax.axis_size("tp")
    shard = lax.axis_index("tp")
    rows = first_ref.shape[0]
    share_of(whole_rows(blocks_ref, shards, shard), own_ref)
    hidden = jnp.concatenate([whole_rows(blocks_ref, shards, k) for k in range(shards)], axis=1)
    squares = lane_squares(hidden)
    scaled = (hidden * gain_ref[...].astype(jnp.float32)).astype(jnp.bfloat16)
    squares = jnp.sum(squares, axis=1, keepdims=True)
    inverse = lax.rsqrt(squares * (1.0 / width) + epsilon)
    pair = (dot(scaled, pair_ref[...]) * inverse).astype(jnp.bfloat16)
    both = jnp.where(lax.axis_index("section") == 0, first_ref[...], pair).astype(jnp.float32)
    share = entry_ref.shape[1]
    offset = shard % (shards // KV_HEADS) * share
    both = pltpu.roll(both, (2 * HEAD - offset) % (2 * HEAD), 1)
    entry_ref[...] = both[:, :share].astype(jnp.bfloat16)
    leave = pltpu.make_async_copy(entry_ref, entry_hbm, sem)
    leave.start()
    query = (dot(scaled, question_ref[...]) * inverse).astype(jnp.bfloat16)
    mixed = attend(query, pair, keys_ref[...], values_ref[...], visible_ref[...])
    store_terms(mixed, back_ref[...], terms_ref)
    leave.wait()


def in_hbm(*arrays):
    return [pltpu.with_memory_space_constraint(a, pltpu.HBM) for a in arrays]


def specs(kinds):
    spaces = {"s": pltpu.SMEM, "v": pltpu.VMEM, "h": pltpu.HBM}
    return [pl.BlockSpec(memory_space=spaces[kind]) for kind in kinds]


def first_layer(terms_shape, parents, extents, warmth, hidden, gain, question, pair, back, address, content):
    rows, width = hidden.shape
    slots = address.shape[2]
    bf16 = functools.partial(jax.ShapeDtypeStruct, dtype=jnp.bfloat16)
    return pl.pallas_call(
        first_layer_kernel,
        out_shape=(
            bf16(terms_shape),
            bf16((rows, 2 * HEAD)),
            jax.ShapeDtypeStruct(terms_shape[1:], jnp.float32),
            bf16((1, width)),
            bf16((width, HEAD)),
            bf16((width, 2 * HEAD)),
            bf16((HEAD, width)),
            bf16((rows * slots, HEAD)),
            bf16((rows * slots, HEAD)),
            jax.ShapeDtypeStruct((rows, HEAD), jnp.int32),
            jax.ShapeDtypeStruct((rows, HEAD), jnp.float32),
        ),
        in_specs=specs("h" * 10),
        out_specs=specs("v" * 11),
        scratch_shapes=[
            pltpu.SMEM((rows,), jnp.int32),
            pltpu.SMEM((rows,), jnp.int32),
            pltpu.SMEM((rows,), jnp.float32),
            pltpu.VMEM((rows, width), jnp.bfloat16),
            pltpu.VMEM((rows, slots, HEAD), jnp.bfloat16),
            pltpu.VMEM((rows, slots, HEAD), jnp.bfloat16),
            pltpu.SemaphoreType.DMA((8,)),
            pltpu.SemaphoreType.DMA((STEPS,)),
            pltpu.SemaphoreType.DMA((STEPS,)),
        ],
        compiler_params=pltpu.CompilerParams(vmem_limit_bytes=LIMIT),
        name="first_layer",
    )(*in_hbm(parents, extents, warmth, hidden, gain, question, pair, back, address, content))


def next_layer(blocks, first, held, share):
    rows = first.shape[0]
    bf16 = functools.partial(jax.ShapeDtypeStruct, dtype=jnp.bfloat16)
    return pl.pallas_call(
        next_layer_kernel,
        out_shape=(
            bf16(blocks.shape),
            bf16((rows, share)),
            jax.ShapeDtypeStruct(blocks.shape[1:], jnp.float32),
        ),
        in_specs=specs("v" * (2 + len(held))),
        out_specs=specs("vhv"),
        scratch_shapes=[pltpu.VMEM((rows, share), jnp.bfloat16), pltpu.SemaphoreType.DMA],
        compiler_params=pltpu.CompilerParams(vmem_limit_bytes=LIMIT),
        name="next_layer",
    )(blocks, first, *held)


def stats_kernel(
    blocks_ref,
    gain_ref,
    warmth_ref,
    noise_ref,
    lexicon_ref,
    out_ref,
    final_hbm,
    final_ref,
    sem,
):
    rows, width = final_ref.shape
    shards = width // HEAD
    squares = jnp.zeros((rows, HEAD), jnp.float32)
    pieces = []
    for k in range(shards):
        hidden = whole_rows(blocks_ref, shards, k)
        final_ref[:, k * HEAD : (k + 1) * HEAD] = hidden.astype(jnp.bfloat16)
        squares = squares + hidden * hidden
        pieces.append((hidden * gain_ref[k : k + 1].astype(jnp.float32)).astype(jnp.bfloat16))
    leave = pltpu.make_async_copy(final_ref, final_hbm, sem)
    leave.start()
    logits = dot(jnp.concatenate(pieces, axis=1), lexicon_ref[...], ((1,), (1,)))
    squares = jnp.sum(squares, axis=1, keepdims=True)
    inverse = lax.rsqrt(squares * (1.0 / width) + epsilon)
    tempered = logits * inverse / warmth_ref[:, :1]
    best = jnp.max(tempered + noise_ref[...], axis=1, keepdims=True)
    peak = jnp.max(tempered, axis=1, keepdims=True)
    mass = jnp.sum(jnp.exp(tempered - peak), axis=1, keepdims=True)
    norm = peak + jnp.log(mass)
    lane = lax.broadcasted_iota(jnp.int32, (rows, HEAD), 1)
    row = lax.broadcasted_iota(jnp.int32, (rows, HEAD), 0)
    packed = jnp.where(lane == row, best, 0.0)
    packed = jnp.where(lane == row + rows, norm, packed)
    packed = jnp.sum(packed, axis=0, keepdims=True)
    out_ref[...] = jnp.broadcast_to(packed[None], out_ref.shape)
    leave.wait()


def local_stats(blocks, gain, warmth, noise, lexicon):
    rows = warmth.shape[0]
    width = lexicon.shape[1]
    return pl.pallas_call(
        stats_kernel,
        out_shape=(
            jax.ShapeDtypeStruct((blocks.shape[0], 1, HEAD), jnp.float32),
            jax.ShapeDtypeStruct((rows, width), jnp.bfloat16),
        ),
        in_specs=specs("vvvvv"),
        out_specs=tuple(specs("vh")),
        scratch_shapes=[
            pltpu.VMEM((rows, width), jnp.bfloat16),
            pltpu.SemaphoreType.DMA,
        ],
        compiler_params=pltpu.CompilerParams(vmem_limit_bytes=LIMIT),
        name="local_stats",
    )(blocks, gain, warmth, noise, lexicon)


def combine_kernel(stats_ref, best_hbm, norm_hbm, best_ref, norm_ref, sems):
    rows = best_ref.shape[0]
    stats = stats_ref[...]
    highest = jnp.max(stats, axis=0)
    norm = highest + jnp.log(jnp.sum(jnp.exp(stats - highest[None]), axis=0))
    best_ref[...] = highest[0, :rows]
    norm_ref[...] = norm[0, rows : 2 * rows]
    copies = [
        pltpu.make_async_copy(best_ref, best_hbm, sems.at[0]),
        pltpu.make_async_copy(norm_ref, norm_hbm, sems.at[1]),
    ]
    for copy in copies:
        copy.start()
    for copy in copies:
        copy.wait()


def combine(stats, rows):
    row = jax.ShapeDtypeStruct((rows,), jnp.float32)
    return pl.pallas_call(
        combine_kernel,
        out_shape=(row, row),
        in_specs=specs("v"),
        out_specs=specs("hh"),
        compiler_params=pltpu.CompilerParams(vmem_limit_bytes=LIMIT // 4),
        scratch_shapes=[
            pltpu.VMEM((rows,), jnp.float32),
            pltpu.VMEM((rows,), jnp.float32),
            pltpu.SemaphoreType.DMA((2,)),
        ],
        name="combine",
    )(stats)


def per_device(
    incoming_hidden_states,
    parent_positions,
    filled_extents,
    stored_address_tensor,
    stored_content_tensor,
    layer_scale_factors,
    question_matrix,
    address_content_matrix,
    projection_back_matrix,
    ending_scale_factors,
    lexicon_matrix,
    sampling_warmth,
    sampling_noise,
):
    shards = lax.axis_size("tp")
    sections = lax.axis_size("section")
    rows, width = incoming_hidden_states.shape
    share = address_content_matrix.shape[2] // shards
    terms_shape = (sections * shards, rows // sections, width // shards)

    def exchange(terms, own, source):
        terms = lax.all_to_all(terms, ("section", "tp"), 0, 0)
        terms = terms[source * shards : (source + 1) * shards]
        block = (own + jnp.sum(terms.astype(jnp.float32), axis=0)).astype(jnp.bfloat16)
        copies = jnp.broadcast_to(block, terms_shape)
        return lax.all_to_all(copies, ("section", "tp"), 0, 0)

    terms, first, own, *held, warmth = first_layer(
        terms_shape,
        parent_positions,
        filled_extents,
        sampling_warmth,
        incoming_hidden_states,
        layer_scale_factors,
        question_matrix,
        address_content_matrix,
        projection_back_matrix,
        stored_address_tensor,
        stored_content_tensor,
    )
    blocks = exchange(terms, own, 0)
    terms, entry, own = next_layer(blocks, first, held, share)
    blocks = exchange(terms, own, 1)
    stats, final_rows = local_stats(
        blocks,
        ending_scale_factors.reshape(width // HEAD, HEAD),
        warmth,
        sampling_noise,
        lexicon_matrix,
    )
    stats = lax.all_to_all(stats, ("section", "tp"), 0, 0)
    best_score, log_norm = combine(stats, rows)
    return (entry[None], final_rows, best_score, log_norm)


def solution(mesh):
    in_specs = (
        P(),
        P(),
        P(),
        P("section", None, None, None),
        P("section", None, None, None),
        P("section", None),
        P("section", None, "tp"),
        P("section", None, None),
        P("section", "tp", None),
        P(),
        P(("section", "tp"), None),
        P(),
        P(None, ("section", "tp")),
    )
    out_specs = (P("section", None, "tp"), P(), P(), P())
    return jax.shard_map(
        per_device, mesh=mesh, in_specs=in_specs, out_specs=out_specs, check_vma=False
    )
```

```python
import functools

import jax
import jax.numpy as jnp
from jax import lax
from jax.experimental import pallas as pl
from jax.experimental.pallas import tpu as pltpu
from jax.sharding import PartitionSpec as P

HEAD = 128
KV_HEADS = 8
STEPS = 4
LIMIT = 16 * 1024 * 1024


epsilon = 1e-05


def dot(a, b, contract=((1,), (0,))):
    return lax.dot_general(a, b, (contract, ((), ())), preferred_element_type=jnp.float32)


def weights_of(width, pieces):
    step = width // pieces
    return [(i * step, step) for i in range(pieces)]


def column_of(scalars, rows):
    row = lax.broadcasted_iota(jnp.int32, (rows, HEAD), 0)
    column = jnp.zeros((rows, HEAD), scalars[0].dtype)
    for j in range(rows):
        column = jnp.where(row == j, scalars[j], column)
    return column


def attend(query, pair, keys, values, visible_slots):
    rows = query.shape[0]
    slots = keys.shape[0] // rows
    new_key = pair[:, :HEAD].astype(jnp.float32)
    new_value = pair[:, HEAD:].astype(jnp.float32)
    score_scale = HEAD ** (-0.5)
    row = lax.broadcasted_iota(jnp.int32, (rows, rows * slots), 0)
    column = lax.broadcasted_iota(jnp.int32, (rows, rows * slots), 1)
    slot = column - row * slots
    visible = (slot >= 0) & (slot < visible_slots[:, :1])
    scores = dot(query, keys, ((1,), (1,))) * score_scale
    own_score = jnp.sum(query.astype(jnp.float32) * new_key, axis=1, keepdims=True) * score_scale
    highest = jnp.maximum(
        jnp.max(jnp.where(visible, scores, -1e30), axis=1, keepdims=True), own_score
    )
    spread = jnp.where(visible, jnp.exp(scores - highest), 0.0)
    own_weight = jnp.exp(own_score - highest)
    denominator = jnp.sum(spread, axis=1, keepdims=True) + own_weight
    probabilities = (spread / denominator).astype(jnp.bfloat16)
    own_prob = (own_weight / denominator).astype(jnp.bfloat16).astype(jnp.float32)
    mixed = dot(probabilities, values) + own_prob * new_value
    return mixed.astype(jnp.bfloat16)


def store_terms(mixed, back, terms_ref):
    terms = dot(mixed, back)
    rows = terms_ref.shape[1]
    parts = mixed.shape[0] // rows
    shards = terms_ref.shape[0] // parts
    for k in range(back.shape[1] // HEAD):
        for p in range(parts):
            block = terms[p * rows : (p + 1) * rows, k * HEAD : (k + 1) * HEAD]
            terms_ref[p * shards + k] = block.astype(jnp.bfloat16)


def lane_squares(hidden):
    total = hidden[:, :HEAD] * hidden[:, :HEAD]
    for k in range(HEAD, hidden.shape[1], HEAD):
        total = total + hidden[:, k : k + HEAD] * hidden[:, k : k + HEAD]
    return total


def share_of(block, own_ref):
    rows = own_ref.shape[0]
    own = block[:rows]
    for p in range(1, block.shape[0] // rows):
        own = jnp.where(lax.axis_index("section") == p, block[p * rows : (p + 1) * rows], own)
    own_ref[...] = own


def whole_rows(blocks_ref, shards, k):
    parts = [blocks_ref[i + k].astype(jnp.float32) for i in range(0, blocks_ref.shape[0], shards)]
    return jnp.concatenate(parts, axis=0)


def first_layer_kernel(
    parents_hbm,
    extents_hbm,
    warmth_hbm,
    hidden_hbm,
    gain_hbm,
    question_hbm,
    pair_hbm,
    back_hbm,
    address_hbm,
    content_hbm,
    terms_ref,
    entry_ref,
    own_ref,
    gain_ref,
    question_ref,
    pair_ref,
    back_ref,
    keys_ref,
    values_ref,
    visible_ref,
    warmth_ref,
    parents,
    extents,
    warmth,
    hidden_ref,
    address_ref,
    content_ref,
    sems,
    question_sems,
    pair_sems,
):
    rows, width = hidden_ref.shape
    slots = address_ref.shape[1]
    shard = lax.axis_index("tp")
    group = shard // (lax.axis_size("tp") // KV_HEADS)
    head_columns = pl.ds(pl.multiple_of(group * HEAD, HEAD), HEAD)
    pair_columns = pl.ds(pl.multiple_of(group * 2 * HEAD, 2 * HEAD), 2 * HEAD)
    small = [
        pltpu.make_async_copy(hidden_hbm, hidden_ref, sems.at[0]),
        pltpu.make_async_copy(gain_hbm, gain_ref, sems.at[1]),
        pltpu.make_async_copy(parents_hbm, parents, sems.at[4]),
        pltpu.make_async_copy(extents_hbm, extents, sems.at[5]),
        pltpu.make_async_copy(warmth_hbm, warmth, sems.at[7]),
    ]
    lines = [
        pltpu.make_async_copy(address_hbm.at[0, :, :, head_columns], address_ref, sems.at[2]),
        pltpu.make_async_copy(content_hbm.at[0, :, :, head_columns], content_ref, sems.at[3]),
    ]
    projections = []
    for i, (start, step) in enumerate(weights_of(width, STEPS)):
        part = pl.ds(start, step)
        projections.append(
            (
                pltpu.make_async_copy(question_hbm.at[0, part], question_ref.at[part], question_sems.at[i]),
                pltpu.make_async_copy(pair_hbm.at[0, part, pair_columns], pair_ref.at[part], pair_sems.at[i]),
            )
        )
    back = pltpu.make_async_copy(back_hbm.at[0], back_ref, sems.at[6])
    for copy in small:
        copy.start()
    for i, two in enumerate(projections):
        for copy in two:
            copy.start()
        if i == 0:
            for copy in lines:
                copy.start()
    back.start()

    for copy in small:
        copy.wait()
    own = hidden_ref[:, pl.ds(pl.multiple_of(shard * HEAD, HEAD), HEAD)]
    share_of(own.astype(jnp.float32), own_ref)
    squares = jnp.zeros((rows, HEAD), jnp.float32)
    query = jnp.zeros((rows, HEAD), jnp.float32)
    pair = jnp.zeros((rows, 2 * HEAD), jnp.float32)
    for i, (start, step) in enumerate(weights_of(width, STEPS)):
        part = slice(start, start + step)
        hidden = hidden_ref[:, part].astype(jnp.float32)
        squares = squares + lane_squares(hidden)
        scaled = (hidden * gain_ref[:, part].astype(jnp.float32)).astype(jnp.bfloat16)
        if i == STEPS // 2:
            visible = column_of([extents[parents[j]] for j in range(rows)], rows)
            visible_ref[...] = visible
            warmth_ref[...] = column_of([warmth[j] for j in range(rows)], rows)
            for copy in lines:
                copy.wait()
            for j in range(rows):
                lines_j = pl.ds(j * slots, slots)
                keys_ref[lines_j] = address_ref[parents[j]]
                values_ref[lines_j] = content_ref[parents[j]]
        for copy in projections[i]:
            copy.wait()
        query = query + dot(scaled, question_ref[part])
        pair = pair + dot(scaled, pair_ref[part])
    squares = jnp.sum(squares, axis=1, keepdims=True)
    inverse = lax.rsqrt(squares * (1.0 / width) + epsilon)
    query = (query * inverse).astype(jnp.bfloat16)
    pair = (pair * inverse).astype(jnp.bfloat16)
    entry_ref[...] = pair
    mixed = attend(query, pair, keys_ref[...], values_ref[...], visible)
    back.wait()
    store_terms(mixed, back_ref[...], terms_ref)


def next_layer_kernel(
    blocks_ref,
    first_ref,
    gain_ref,
    question_ref,
    pair_ref,
    back_ref,
    keys_ref,
    values_ref,
    visible_ref,
    terms_ref,
    entry_hbm,
    own_ref,
    entry_ref,
    sem,
):
    width = question_ref.shape[0]
    shards = lax.axis_size("tp")
    shard = lax.axis_index("tp")
    rows = first_ref.shape[0]
    share_of(whole_rows(blocks_ref, shards, shard), own_ref)
    hidden = jnp.concatenate([whole_rows(blocks_ref, shards, k) for k in range(shards)], axis=1)
    squares = lane_squares(hidden)
    scaled = (hidden * gain_ref[...].astype(jnp.float32)).astype(jnp.bfloat16)
    squares = jnp.sum(squares, axis=1, keepdims=True)
    inverse = lax.rsqrt(squares * (1.0 / width) + epsilon)
    pair = (dot(scaled, pair_ref[...]) * inverse).astype(jnp.bfloat16)
    both = jnp.where(lax.axis_index("section") == 0, first_ref[...], pair).astype(jnp.float32)
    share = entry_ref.shape[1]
    offset = shard % (shards // KV_HEADS) * share
    both = pltpu.roll(both, (2 * HEAD - offset) % (2 * HEAD), 1)
    entry_ref[...] = both[:, :share].astype(jnp.bfloat16)
    leave = pltpu.make_async_copy(entry_ref, entry_hbm, sem)
    leave.start()
    query = (dot(scaled, question_ref[...]) * inverse).astype(jnp.bfloat16)
    mixed = attend(query, pair, keys_ref[...], values_ref[...], visible_ref[...])
    store_terms(mixed, back_ref[...], terms_ref)
    leave.wait()


def in_hbm(*arrays):
    return [pltpu.with_memory_space_constraint(a, pltpu.HBM) for a in arrays]


def specs(kinds):
    spaces = {"s": pltpu.SMEM, "v": pltpu.VMEM, "h": pltpu.HBM}
    return [pl.BlockSpec(memory_space=spaces[kind]) for kind in kinds]


def first_layer(terms_shape, parents, extents, warmth, hidden, gain, question, pair, back, address, content):
    rows, width = hidden.shape
    slots = address.shape[2]
    bf16 = functools.partial(jax.ShapeDtypeStruct, dtype=jnp.bfloat16)
    return pl.pallas_call(
        first_layer_kernel,
        out_shape=(
            bf16(terms_shape),
            bf16((rows, 2 * HEAD)),
            jax.ShapeDtypeStruct(terms_shape[1:], jnp.float32),
            bf16((1, width)),
            bf16((width, HEAD)),
            bf16((width, 2 * HEAD)),
            bf16((HEAD, width)),
            bf16((rows * slots, HEAD)),
            bf16((rows * slots, HEAD)),
            jax.ShapeDtypeStruct((rows, HEAD), jnp.int32),
            jax.ShapeDtypeStruct((rows, HEAD), jnp.float32),
        ),
        in_specs=specs("h" * 10),
        out_specs=specs("v" * 11),
        scratch_shapes=[
            pltpu.SMEM((rows,), jnp.int32),
            pltpu.SMEM((rows,), jnp.int32),
            pltpu.SMEM((rows,), jnp.float32),
            pltpu.VMEM((rows, width), jnp.bfloat16),
            pltpu.VMEM((rows, slots, HEAD), jnp.bfloat16),
            pltpu.VMEM((rows, slots, HEAD), jnp.bfloat16),
            pltpu.SemaphoreType.DMA((8,)),
            pltpu.SemaphoreType.DMA((STEPS,)),
            pltpu.SemaphoreType.DMA((STEPS,)),
        ],
        compiler_params=pltpu.CompilerParams(vmem_limit_bytes=LIMIT),
        name="first_layer",
    )(*in_hbm(parents, extents, warmth, hidden, gain, question, pair, back, address, content))


def next_layer(blocks, first, held, share):
    rows = first.shape[0]
    bf16 = functools.partial(jax.ShapeDtypeStruct, dtype=jnp.bfloat16)
    return pl.pallas_call(
        next_layer_kernel,
        out_shape=(
            bf16(blocks.shape),
            bf16((rows, share)),
            jax.ShapeDtypeStruct(blocks.shape[1:], jnp.float32),
        ),
        in_specs=specs("v" * (2 + len(held))),
        out_specs=specs("vhv"),
        scratch_shapes=[pltpu.VMEM((rows, share), jnp.bfloat16), pltpu.SemaphoreType.DMA],
        compiler_params=pltpu.CompilerParams(vmem_limit_bytes=LIMIT),
        name="next_layer",
    )(blocks, first, *held)


def stats_kernel(blocks_ref, gain_ref, warmth_ref, noise_ref, lexicon_ref, out_ref, final_ref):
    rows, width = final_ref.shape
    shards = width // HEAD
    squares = jnp.zeros((rows, HEAD), jnp.float32)
    pieces = []
    for k in range(shards):
        hidden = whole_rows(blocks_ref, shards, k)
        final_ref[:, k * HEAD : (k + 1) * HEAD] = hidden.astype(jnp.bfloat16)
        squares = squares + hidden * hidden
        pieces.append((hidden * gain_ref[k : k + 1].astype(jnp.float32)).astype(jnp.bfloat16))
    logits = dot(jnp.concatenate(pieces, axis=1), lexicon_ref[...], ((1,), (1,)))
    squares = jnp.sum(squares, axis=1, keepdims=True)
    inverse = lax.rsqrt(squares * (1.0 / width) + epsilon)
    tempered = logits * inverse / warmth_ref[:, :1]
    best = jnp.max(tempered + noise_ref[...], axis=1, keepdims=True)
    peak = jnp.max(tempered, axis=1, keepdims=True)
    mass = jnp.sum(jnp.exp(tempered - peak), axis=1, keepdims=True)
    norm = peak + jnp.log(mass)
    lane = lax.broadcasted_iota(jnp.int32, (rows, HEAD), 1)
    row = lax.broadcasted_iota(jnp.int32, (rows, HEAD), 0)
    packed = jnp.where(lane == row, best, 0.0)
    packed = jnp.where(lane == row + rows, norm, packed)
    packed = jnp.sum(packed, axis=0, keepdims=True)
    out_ref[...] = jnp.broadcast_to(packed[None], out_ref.shape)


def local_stats(blocks, gain, warmth, noise, lexicon):
    rows = warmth.shape[0]
    width = lexicon.shape[1]
    return pl.pallas_call(
        stats_kernel,
        out_shape=(
            jax.ShapeDtypeStruct((blocks.shape[0], 1, HEAD), jnp.float32),
            pltpu.VMEM((rows, width), jnp.bfloat16),
        ),
        in_specs=specs("vvvvv"),
        out_specs=tuple(specs("vv")),
        compiler_params=pltpu.CompilerParams(vmem_limit_bytes=LIMIT),
        name="local_stats",
    )(blocks, gain, warmth, noise, lexicon)


def combine_kernel(
    stats_ref, final_ref, best_hbm, norm_hbm, final_hbm, best_ref, norm_ref, sems
):
    leave = pltpu.make_async_copy(final_ref, final_hbm, sems.at[2])
    leave.start()
    rows = best_ref.shape[0]
    stats = stats_ref[...]
    highest = jnp.max(stats, axis=0)
    norm = highest + jnp.log(jnp.sum(jnp.exp(stats - highest[None]), axis=0))
    best_ref[...] = highest[0, :rows]
    norm_ref[...] = norm[0, rows : 2 * rows]
    copies = [
        pltpu.make_async_copy(best_ref, best_hbm, sems.at[0]),
        pltpu.make_async_copy(norm_ref, norm_hbm, sems.at[1]),
    ]
    for copy in copies:
        copy.start()
    for copy in copies:
        copy.wait()
    leave.wait()


def combine(stats, final):
    rows = final.shape[0]
    row = jax.ShapeDtypeStruct((rows,), jnp.float32)
    return pl.pallas_call(
        combine_kernel,
        out_shape=(row, row, jax.ShapeDtypeStruct(final.shape, final.dtype)),
        in_specs=specs("vv"),
        out_specs=specs("hhh"),
        scratch_shapes=[
            pltpu.VMEM((rows,), jnp.float32),
            pltpu.VMEM((rows,), jnp.float32),
            pltpu.SemaphoreType.DMA((3,)),
        ],
        compiler_params=pltpu.CompilerParams(vmem_limit_bytes=LIMIT // 4),
        name="combine",
    )(stats, pltpu.with_memory_space_constraint(final, pltpu.VMEM))


def per_device(
    incoming_hidden_states,
    parent_positions,
    filled_extents,
    stored_address_tensor,
    stored_content_tensor,
    layer_scale_factors,
    question_matrix,
    address_content_matrix,
    projection_back_matrix,
    ending_scale_factors,
    lexicon_matrix,
    sampling_warmth,
    sampling_noise,
):
    shards = lax.axis_size("tp")
    sections = lax.axis_size("section")
    rows, width = incoming_hidden_states.shape
    share = address_content_matrix.shape[2] // shards
    terms_shape = (sections * shards, rows // sections, width // shards)

    def exchange(terms, own, source):
        terms = lax.all_to_all(terms, ("section", "tp"), 0, 0)
        terms = terms[source * shards : (source + 1) * shards]
        block = (own + jnp.sum(terms.astype(jnp.float32), axis=0)).astype(jnp.bfloat16)
        copies = jnp.broadcast_to(block, terms_shape)
        return lax.all_to_all(copies, ("section", "tp"), 0, 0)

    terms, first, own, *held, warmth = first_layer(
        terms_shape,
        parent_positions,
        filled_extents,
        sampling_warmth,
        incoming_hidden_states,
        layer_scale_factors,
        question_matrix,
        address_content_matrix,
        projection_back_matrix,
        stored_address_tensor,
        stored_content_tensor,
    )
    blocks = exchange(terms, own, 0)
    terms, entry, own = next_layer(blocks, first, held, share)
    blocks = exchange(terms, own, 1)
    stats, final_rows = local_stats(
        blocks,
        ending_scale_factors.reshape(width // HEAD, HEAD),
        warmth,
        sampling_noise,
        lexicon_matrix,
    )
    stats = lax.all_to_all(stats, ("section", "tp"), 0, 0)
    best_score, log_norm, final_rows = combine(stats, final_rows)
    return (entry[None], final_rows, best_score, log_norm)


def solution(mesh):
    in_specs = (
        P(),
        P(),
        P(),
        P("section", None, None, None),
        P("section", None, None, None),
        P("section", None),
        P("section", None, "tp"),
        P("section", None, None),
        P("section", "tp", None),
        P(),
        P(("section", "tp"), None),
        P(),
        P(None, ("section", "tp")),
    )
    out_specs = (P("section", None, "tp"), P(), P(), P())
    return jax.shard_map(
        per_device, mesh=mesh, in_specs=in_specs, out_specs=out_specs, check_vma=False
    )
```

```python
import functools

import jax
import jax.numpy as jnp
from jax import lax
from jax.experimental import pallas as pl
from jax.experimental.pallas import tpu as pltpu
from jax.sharding import PartitionSpec as P

HEAD = 128
KV_HEADS = 8
STEPS = 4
LIMIT = 16 * 1024 * 1024


epsilon = 1e-05


def dot(a, b, contract=((1,), (0,))):
    return lax.dot_general(a, b, (contract, ((), ())), preferred_element_type=jnp.float32)


def weights_of(width, pieces):
    step = width // pieces
    return [(i * step, step) for i in range(pieces)]


def column_of(scalars, rows):
    row = lax.broadcasted_iota(jnp.int32, (rows, HEAD), 0)
    column = jnp.zeros((rows, HEAD), scalars[0].dtype)
    for j in range(rows):
        column = jnp.where(row == j, scalars[j], column)
    return column


def attend(query, pair, keys, values, visible_slots):
    rows = query.shape[0]
    slots = keys.shape[0] // rows
    new_key = pair[:, :HEAD].astype(jnp.float32)
    new_value = pair[:, HEAD:].astype(jnp.float32)
    score_scale = HEAD ** (-0.5)
    row = lax.broadcasted_iota(jnp.int32, (rows, rows * slots), 0)
    column = lax.broadcasted_iota(jnp.int32, (rows, rows * slots), 1)
    slot = column - row * slots
    visible = (slot >= 0) & (slot < visible_slots[:, :1])
    scores = dot(query, keys, ((1,), (1,))) * score_scale
    own_score = jnp.sum(query.astype(jnp.float32) * new_key, axis=1, keepdims=True) * score_scale
    highest = jnp.maximum(
        jnp.max(jnp.where(visible, scores, -1e30), axis=1, keepdims=True), own_score
    )
    spread = jnp.where(visible, jnp.exp(scores - highest), 0.0)
    own_weight = jnp.exp(own_score - highest)
    denominator = jnp.sum(spread, axis=1, keepdims=True) + own_weight
    probabilities = (spread / denominator).astype(jnp.bfloat16)
    own_prob = (own_weight / denominator).astype(jnp.bfloat16).astype(jnp.float32)
    mixed = dot(probabilities, values) + own_prob * new_value
    return mixed.astype(jnp.bfloat16)


def store_terms(mixed, back, terms_ref):
    terms = dot(mixed, back)
    rows = terms_ref.shape[1]
    parts = mixed.shape[0] // rows
    shards = terms_ref.shape[0] // parts
    for k in range(back.shape[1] // HEAD):
        for p in range(parts):
            block = terms[p * rows : (p + 1) * rows, k * HEAD : (k + 1) * HEAD]
            terms_ref[p * shards + k] = block.astype(jnp.bfloat16)


def lane_squares(hidden):
    total = hidden[:, :HEAD] * hidden[:, :HEAD]
    for k in range(HEAD, hidden.shape[1], HEAD):
        total = total + hidden[:, k : k + HEAD] * hidden[:, k : k + HEAD]
    return total


def share_of(block, own_ref):
    rows = own_ref.shape[0]
    own = block[:rows]
    for p in range(1, block.shape[0] // rows):
        own = jnp.where(lax.axis_index("section") == p, block[p * rows : (p + 1) * rows], own)
    own_ref[...] = own


def whole_rows(blocks_ref, shards, k):
    parts = [blocks_ref[i + k].astype(jnp.float32) for i in range(0, blocks_ref.shape[0], shards)]
    return jnp.concatenate(parts, axis=0)


def first_layer_kernel(
    parents_hbm,
    extents_hbm,
    warmth_hbm,
    hidden_hbm,
    gain_hbm,
    question_hbm,
    pair_hbm,
    back_hbm,
    address_hbm,
    content_hbm,
    terms_ref,
    entry_ref,
    own_ref,
    gain_ref,
    question_ref,
    pair_ref,
    back_ref,
    keys_ref,
    values_ref,
    visible_ref,
    warmth_ref,
    parents,
    extents,
    warmth,
    hidden_ref,
    address_ref,
    content_ref,
    sems,
    question_sems,
    pair_sems,
):
    rows, width = hidden_ref.shape
    slots = address_ref.shape[1]
    shard = lax.axis_index("tp")
    group = shard // (lax.axis_size("tp") // KV_HEADS)
    head_columns = pl.ds(pl.multiple_of(group * HEAD, HEAD), HEAD)
    pair_columns = pl.ds(pl.multiple_of(group * 2 * HEAD, 2 * HEAD), 2 * HEAD)
    small = [
        pltpu.make_async_copy(hidden_hbm, hidden_ref, sems.at[0]),
        pltpu.make_async_copy(gain_hbm, gain_ref, sems.at[1]),
        pltpu.make_async_copy(parents_hbm, parents, sems.at[4]),
        pltpu.make_async_copy(extents_hbm, extents, sems.at[5]),
        pltpu.make_async_copy(warmth_hbm, warmth, sems.at[7]),
    ]
    lines = [
        pltpu.make_async_copy(address_hbm.at[0, :, :, head_columns], address_ref, sems.at[2]),
        pltpu.make_async_copy(content_hbm.at[0, :, :, head_columns], content_ref, sems.at[3]),
    ]
    projections = []
    for i, (start, step) in enumerate(weights_of(width, STEPS)):
        part = pl.ds(start, step)
        projections.append(
            (
                pltpu.make_async_copy(question_hbm.at[0, part], question_ref.at[part], question_sems.at[i]),
                pltpu.make_async_copy(pair_hbm.at[0, part, pair_columns], pair_ref.at[part], pair_sems.at[i]),
            )
        )
    back = pltpu.make_async_copy(back_hbm.at[0], back_ref, sems.at[6])
    for copy in small:
        copy.start()
    for i, two in enumerate(projections):
        for copy in two:
            copy.start()
        if i == 0:
            for copy in lines:
                copy.start()
    back.start()

    for copy in small:
        copy.wait()
    own = hidden_ref[:, pl.ds(pl.multiple_of(shard * HEAD, HEAD), HEAD)]
    share_of(own.astype(jnp.float32), own_ref)
    squares = jnp.zeros((rows, HEAD), jnp.float32)
    query = jnp.zeros((rows, HEAD), jnp.float32)
    pair = jnp.zeros((rows, 2 * HEAD), jnp.float32)
    for i, (start, step) in enumerate(weights_of(width, STEPS)):
        part = slice(start, start + step)
        hidden = hidden_ref[:, part].astype(jnp.float32)
        squares = squares + lane_squares(hidden)
        scaled = (hidden * gain_ref[:, part].astype(jnp.float32)).astype(jnp.bfloat16)
        if i == STEPS // 2:
            visible = column_of([extents[parents[j]] for j in range(rows)], rows)
            visible_ref[...] = visible
            warmth_ref[...] = column_of([warmth[j] for j in range(rows)], rows)
            for copy in lines:
                copy.wait()
            for j in range(rows):
                lines_j = pl.ds(j * slots, slots)
                keys_ref[lines_j] = address_ref[parents[j]]
                values_ref[lines_j] = content_ref[parents[j]]
        for copy in projections[i]:
            copy.wait()
        query = query + dot(scaled, question_ref[part])
        pair = pair + dot(scaled, pair_ref[part])
    squares = jnp.sum(squares, axis=1, keepdims=True)
    inverse = lax.rsqrt(squares * (1.0 / width) + epsilon)
    query = (query * inverse).astype(jnp.bfloat16)
    pair = (pair * inverse).astype(jnp.bfloat16)
    entry_ref[...] = pair
    mixed = attend(query, pair, keys_ref[...], values_ref[...], visible)
    back.wait()
    store_terms(mixed, back_ref[...], terms_ref)


def next_layer_kernel(
    blocks_ref,
    first_ref,
    gain_ref,
    question_ref,
    pair_ref,
    back_ref,
    keys_ref,
    values_ref,
    visible_ref,
    terms_ref,
    entry_hbm,
    own_ref,
    entry_ref,
    sem,
):
    width = question_ref.shape[0]
    shards = lax.axis_size("tp")
    shard = lax.axis_index("tp")
    rows = first_ref.shape[0]
    share_of(whole_rows(blocks_ref, shards, shard), own_ref)
    hidden = jnp.concatenate([whole_rows(blocks_ref, shards, k) for k in range(shards)], axis=1)
    squares = lane_squares(hidden)
    scaled = (hidden * gain_ref[...].astype(jnp.float32)).astype(jnp.bfloat16)
    squares = jnp.sum(squares, axis=1, keepdims=True)
    inverse = lax.rsqrt(squares * (1.0 / width) + epsilon)
    pair = (dot(scaled, pair_ref[...]) * inverse).astype(jnp.bfloat16)
    both = jnp.where(lax.axis_index("section") == 0, first_ref[...], pair).astype(jnp.float32)
    share = entry_ref.shape[1]
    offset = shard % (shards // KV_HEADS) * share
    both = pltpu.roll(both, (2 * HEAD - offset) % (2 * HEAD), 1)
    entry_ref[...] = both[:, :share].astype(jnp.bfloat16)
    leave = pltpu.make_async_copy(entry_ref, entry_hbm, sem)
    leave.start()
    query = (dot(scaled, question_ref[...]) * inverse).astype(jnp.bfloat16)
    mixed = attend(query, pair, keys_ref[...], values_ref[...], visible_ref[...])
    store_terms(mixed, back_ref[...], terms_ref)
    leave.wait()


def in_hbm(*arrays):
    return [pltpu.with_memory_space_constraint(a, pltpu.HBM) for a in arrays]


def specs(kinds):
    spaces = {"s": pltpu.SMEM, "v": pltpu.VMEM, "h": pltpu.HBM}
    return [pl.BlockSpec(memory_space=spaces[kind]) for kind in kinds]


def first_layer(terms_shape, parents, extents, warmth, hidden, gain, question, pair, back, address, content):
    rows, width = hidden.shape
    slots = address.shape[2]
    bf16 = functools.partial(jax.ShapeDtypeStruct, dtype=jnp.bfloat16)
    return pl.pallas_call(
        first_layer_kernel,
        out_shape=(
            bf16(terms_shape),
            bf16((rows, 2 * HEAD)),
            jax.ShapeDtypeStruct(terms_shape[1:], jnp.float32),
            bf16((1, width)),
            bf16((width, HEAD)),
            bf16((width, 2 * HEAD)),
            bf16((HEAD, width)),
            bf16((rows * slots, HEAD)),
            bf16((rows * slots, HEAD)),
            jax.ShapeDtypeStruct((rows, HEAD), jnp.int32),
            jax.ShapeDtypeStruct((rows, HEAD), jnp.float32),
        ),
        in_specs=specs("h" * 10),
        out_specs=specs("v" * 11),
        scratch_shapes=[
            pltpu.SMEM((rows,), jnp.int32),
            pltpu.SMEM((rows,), jnp.int32),
            pltpu.SMEM((rows,), jnp.float32),
            pltpu.VMEM((rows, width), jnp.bfloat16),
            pltpu.VMEM((rows, slots, HEAD), jnp.bfloat16),
            pltpu.VMEM((rows, slots, HEAD), jnp.bfloat16),
            pltpu.SemaphoreType.DMA((8,)),
            pltpu.SemaphoreType.DMA((STEPS,)),
            pltpu.SemaphoreType.DMA((STEPS,)),
        ],
        compiler_params=pltpu.CompilerParams(vmem_limit_bytes=LIMIT),
        name="first_layer",
    )(*in_hbm(parents, extents, warmth, hidden, gain, question, pair, back, address, content))


def next_layer(blocks, first, held, share):
    rows = first.shape[0]
    bf16 = functools.partial(jax.ShapeDtypeStruct, dtype=jnp.bfloat16)
    return pl.pallas_call(
        next_layer_kernel,
        out_shape=(
            bf16(blocks.shape),
            bf16((rows, share)),
            jax.ShapeDtypeStruct(blocks.shape[1:], jnp.float32),
        ),
        in_specs=specs("v" * (2 + len(held))),
        out_specs=specs("vhv"),
        scratch_shapes=[pltpu.VMEM((rows, share), jnp.bfloat16), pltpu.SemaphoreType.DMA],
        compiler_params=pltpu.CompilerParams(vmem_limit_bytes=LIMIT),
        name="next_layer",
    )(blocks, first, *held)


def stats_kernel(blocks_ref, gain_ref, warmth_ref, noise_ref, lexicon_ref, out_ref, final_ref):
    rows, width = final_ref.shape
    shards = width // HEAD
    squares = jnp.zeros((rows, HEAD), jnp.float32)
    pieces = []
    for k in range(shards):
        hidden = whole_rows(blocks_ref, shards, k)
        final_ref[:, k * HEAD : (k + 1) * HEAD] = hidden.astype(jnp.bfloat16)
        squares = squares + hidden * hidden
        pieces.append((hidden * gain_ref[k : k + 1].astype(jnp.float32)).astype(jnp.bfloat16))
    logits = dot(jnp.concatenate(pieces, axis=1), lexicon_ref[...], ((1,), (1,)))
    squares = jnp.sum(squares, axis=1, keepdims=True)
    inverse = lax.rsqrt(squares * (1.0 / width) + epsilon)
    tempered = logits * inverse / warmth_ref[:, :1]
    best = jnp.max(tempered + noise_ref[...], axis=1, keepdims=True)
    peak = jnp.max(tempered, axis=1, keepdims=True)
    mass = jnp.sum(jnp.exp(tempered - peak), axis=1, keepdims=True)
    norm = peak + jnp.log(mass)
    lane = lax.broadcasted_iota(jnp.int32, (rows, HEAD), 1)
    row = lax.broadcasted_iota(jnp.int32, (rows, HEAD), 0)
    packed = jnp.where(lane == row, best, 0.0)
    packed = jnp.where(lane == row + rows, norm, packed)
    packed = jnp.sum(packed, axis=0, keepdims=True)
    out_ref[...] = jnp.broadcast_to(packed[None], out_ref.shape)


def local_stats(blocks, gain, warmth, noise, lexicon):
    rows = warmth.shape[0]
    width = lexicon.shape[1]
    return pl.pallas_call(
        stats_kernel,
        out_shape=(
            jax.ShapeDtypeStruct((blocks.shape[0] // 8, 8, HEAD), jnp.float32),
            pltpu.VMEM((rows, width), jnp.bfloat16),
        ),
        in_specs=specs("vvvvv"),
        out_specs=tuple(specs("vv")),
        compiler_params=pltpu.CompilerParams(vmem_limit_bytes=LIMIT),
        name="local_stats",
    )(blocks, gain, warmth, noise, lexicon)


def combine_kernel(
    stats_ref, final_ref, best_hbm, norm_hbm, final_hbm, best_ref, norm_ref, sems
):
    leave = pltpu.make_async_copy(final_ref, final_hbm, sems.at[2])
    leave.start()
    rows = best_ref.shape[0]
    stats = stats_ref[...]
    highest = jnp.max(jnp.max(stats, axis=0), axis=0, keepdims=True)
    mass = jnp.sum(jnp.exp(stats - highest[None]), axis=0)
    norm = highest + jnp.log(jnp.sum(mass, axis=0, keepdims=True))
    best_ref[...] = highest[0, :rows]
    norm_ref[...] = norm[0, rows : 2 * rows]
    copies = [
        pltpu.make_async_copy(best_ref, best_hbm, sems.at[0]),
        pltpu.make_async_copy(norm_ref, norm_hbm, sems.at[1]),
    ]
    for copy in copies:
        copy.start()
    for copy in copies:
        copy.wait()
    leave.wait()


def combine(stats, final):
    rows = final.shape[0]
    row = jax.ShapeDtypeStruct((rows,), jnp.float32)
    return pl.pallas_call(
        combine_kernel,
        out_shape=(row, row, jax.ShapeDtypeStruct(final.shape, final.dtype)),
        in_specs=specs("vv"),
        out_specs=specs("hhh"),
        scratch_shapes=[
            pltpu.VMEM((rows,), jnp.float32),
            pltpu.VMEM((rows,), jnp.float32),
            pltpu.SemaphoreType.DMA((3,)),
        ],
        compiler_params=pltpu.CompilerParams(vmem_limit_bytes=LIMIT // 4),
        name="combine",
    )(stats, pltpu.with_memory_space_constraint(final, pltpu.VMEM))


def per_device(
    incoming_hidden_states,
    parent_positions,
    filled_extents,
    stored_address_tensor,
    stored_content_tensor,
    layer_scale_factors,
    question_matrix,
    address_content_matrix,
    projection_back_matrix,
    ending_scale_factors,
    lexicon_matrix,
    sampling_warmth,
    sampling_noise,
):
    shards = lax.axis_size("tp")
    sections = lax.axis_size("section")
    rows, width = incoming_hidden_states.shape
    share = address_content_matrix.shape[2] // shards
    terms_shape = (sections * shards, rows // sections, width // shards)

    def exchange(terms, own, source):
        terms = lax.all_to_all(terms, ("section", "tp"), 0, 0)
        terms = terms[source * shards : (source + 1) * shards]
        block = (own + jnp.sum(terms.astype(jnp.float32), axis=0)).astype(jnp.bfloat16)
        copies = jnp.broadcast_to(block, terms_shape)
        return lax.all_to_all(copies, ("section", "tp"), 0, 0)

    terms, first, own, *held, warmth = first_layer(
        terms_shape,
        parent_positions,
        filled_extents,
        sampling_warmth,
        incoming_hidden_states,
        layer_scale_factors,
        question_matrix,
        address_content_matrix,
        projection_back_matrix,
        stored_address_tensor,
        stored_content_tensor,
    )
    blocks = exchange(terms, own, 0)
    terms, entry, own = next_layer(blocks, first, held, share)
    blocks = exchange(terms, own, 1)
    stats, final_rows = local_stats(
        blocks,
        ending_scale_factors.reshape(width // HEAD, HEAD),
        warmth,
        sampling_noise,
        lexicon_matrix,
    )
    stats = lax.all_to_all(stats.reshape(sections * shards, 1, HEAD), ("section", "tp"), 0, 0)
    stats = stats.reshape(sections * shards // 8, 8, HEAD)
    best_score, log_norm, final_rows = combine(stats, final_rows)
    return (entry[None], final_rows, best_score, log_norm)


def solution(mesh):
    in_specs = (
        P(),
        P(),
        P(),
        P("section", None, None, None),
        P("section", None, None, None),
        P("section", None),
        P("section", None, "tp"),
        P("section", None, None),
        P("section", "tp", None),
        P(),
        P(("section", "tp"), None),
        P(),
        P(None, ("section", "tp")),
    )
    out_specs = (P("section", None, "tp"), P(), P(), P())
    return jax.shard_map(
        per_device, mesh=mesh, in_specs=in_specs, out_specs=out_specs, check_vma=False
    )
```

```python
import functools

import jax
import jax.numpy as jnp
from jax import lax
from jax.experimental import pallas as pl
from jax.experimental.pallas import tpu as pltpu
from jax.sharding import PartitionSpec as P

HEAD = 128
KV_HEADS = 8
STEPS = 4
LIMIT = 16 * 1024 * 1024


epsilon = 1e-05


def dot(a, b, contract=((1,), (0,))):
    return lax.dot_general(a, b, (contract, ((), ())), preferred_element_type=jnp.float32)


def weights_of(width, pieces):
    step = width // pieces
    return [(i * step, step) for i in range(pieces)]


def column_of(scalars, rows):
    row = lax.broadcasted_iota(jnp.int32, (rows, HEAD), 0)
    column = jnp.zeros((rows, HEAD), scalars[0].dtype)
    for j in range(rows):
        column = jnp.where(row == j, scalars[j], column)
    return column


def mask_of(visible_slots, rows, slots):
    row = lax.broadcasted_iota(jnp.int32, (rows, rows * slots), 0)
    column = lax.broadcasted_iota(jnp.int32, (rows, rows * slots), 1)
    slot = column - row * slots
    return ((slot >= 0) & (slot < visible_slots[:, :1])).astype(jnp.int32)


def attend(query, pair, keys, values, mask):
    new_key = pair[:, :HEAD].astype(jnp.float32)
    new_value = pair[:, HEAD:].astype(jnp.float32)
    score_scale = HEAD ** (-0.5)
    visible = mask != 0
    scores = dot(query, keys, ((1,), (1,))) * score_scale
    own_score = jnp.sum(query.astype(jnp.float32) * new_key, axis=1, keepdims=True) * score_scale
    highest = jnp.maximum(
        jnp.max(jnp.where(visible, scores, -1e30), axis=1, keepdims=True), own_score
    )
    spread = jnp.where(visible, jnp.exp(scores - highest), 0.0)
    own_weight = jnp.exp(own_score - highest)
    denominator = jnp.sum(spread, axis=1, keepdims=True) + own_weight
    share = 1.0 / denominator
    probabilities = (spread * share).astype(jnp.bfloat16)
    own_prob = (own_weight * share).astype(jnp.bfloat16).astype(jnp.float32)
    mixed = dot(probabilities, values) + own_prob * new_value
    return mixed.astype(jnp.bfloat16)


def store_terms(mixed, back, terms_ref):
    terms = dot(mixed, back)
    rows = terms_ref.shape[1]
    parts = mixed.shape[0] // rows
    shards = terms_ref.shape[0] // parts
    for k in range(back.shape[1] // HEAD):
        for p in range(parts):
            block = terms[p * rows : (p + 1) * rows, k * HEAD : (k + 1) * HEAD]
            terms_ref[p * shards + k] = block.astype(jnp.bfloat16)


def lane_squares(hidden):
    total = hidden[:, :HEAD] * hidden[:, :HEAD]
    for k in range(HEAD, hidden.shape[1], HEAD):
        total = total + hidden[:, k : k + HEAD] * hidden[:, k : k + HEAD]
    return total


def share_of(block, own_ref):
    rows = own_ref.shape[0]
    own = block[:rows]
    for p in range(1, block.shape[0] // rows):
        own = jnp.where(lax.axis_index("section") == p, block[p * rows : (p + 1) * rows], own)
    own_ref[...] = own


def whole_rows(blocks_ref, shards, k):
    parts = [blocks_ref[i + k].astype(jnp.float32) for i in range(0, blocks_ref.shape[0], shards)]
    return jnp.concatenate(parts, axis=0)


def first_layer_kernel(
    parents_hbm,
    extents_hbm,
    warmth_hbm,
    hidden_hbm,
    gain_hbm,
    question_hbm,
    pair_hbm,
    back_hbm,
    address_hbm,
    content_hbm,
    terms_ref,
    entry_ref,
    own_ref,
    gain_ref,
    question_ref,
    pair_ref,
    back_ref,
    keys_ref,
    values_ref,
    visible_ref,
    warmth_ref,
    parents,
    extents,
    warmth,
    hidden_ref,
    address_ref,
    content_ref,
    sems,
    question_sems,
    pair_sems,
):
    rows, width = hidden_ref.shape
    slots = address_ref.shape[1]
    shard = lax.axis_index("tp")
    group = shard // (lax.axis_size("tp") // KV_HEADS)
    head_columns = pl.ds(pl.multiple_of(group * HEAD, HEAD), HEAD)
    pair_columns = pl.ds(pl.multiple_of(group * 2 * HEAD, 2 * HEAD), 2 * HEAD)
    small = [
        pltpu.make_async_copy(hidden_hbm, hidden_ref, sems.at[0]),
        pltpu.make_async_copy(gain_hbm, gain_ref, sems.at[1]),
        pltpu.make_async_copy(parents_hbm, parents, sems.at[4]),
        pltpu.make_async_copy(extents_hbm, extents, sems.at[5]),
        pltpu.make_async_copy(warmth_hbm, warmth, sems.at[7]),
    ]
    lines = [
        pltpu.make_async_copy(address_hbm.at[0, :, :, head_columns], address_ref, sems.at[2]),
        pltpu.make_async_copy(content_hbm.at[0, :, :, head_columns], content_ref, sems.at[3]),
    ]
    projections = []
    for i, (start, step) in enumerate(weights_of(width, STEPS)):
        part = pl.ds(start, step)
        projections.append(
            (
                pltpu.make_async_copy(question_hbm.at[0, part], question_ref.at[part], question_sems.at[i]),
                pltpu.make_async_copy(pair_hbm.at[0, part, pair_columns], pair_ref.at[part], pair_sems.at[i]),
            )
        )
    back = pltpu.make_async_copy(back_hbm.at[0], back_ref, sems.at[6])
    for copy in small:
        copy.start()
    for i, two in enumerate(projections):
        for copy in two:
            copy.start()
        if i == 0:
            for copy in lines:
                copy.start()
    back.start()

    for copy in small:
        copy.wait()
    own = hidden_ref[:, pl.ds(pl.multiple_of(shard * HEAD, HEAD), HEAD)]
    share_of(own.astype(jnp.float32), own_ref)
    squares = jnp.zeros((rows, HEAD), jnp.float32)
    query = jnp.zeros((rows, HEAD), jnp.float32)
    pair = jnp.zeros((rows, 2 * HEAD), jnp.float32)
    for i, (start, step) in enumerate(weights_of(width, STEPS)):
        part = slice(start, start + step)
        hidden = hidden_ref[:, part].astype(jnp.float32)
        squares = squares + lane_squares(hidden)
        scaled = (hidden * gain_ref[:, part].astype(jnp.float32)).astype(jnp.bfloat16)
        if i == STEPS // 2:
            limits = column_of([extents[parents[j]] for j in range(rows)], rows)
            visible = mask_of(limits, rows, slots)
            visible_ref[...] = visible
            warmth_ref[...] = column_of([warmth[j] for j in range(rows)], rows)
            for copy in lines:
                copy.wait()
            for j in range(rows):
                lines_j = pl.ds(j * slots, slots)
                keys_ref[lines_j] = address_ref[parents[j]]
                values_ref[lines_j] = content_ref[parents[j]]
        for copy in projections[i]:
            copy.wait()
        query = query + dot(scaled, question_ref[part])
        pair = pair + dot(scaled, pair_ref[part])
    squares = jnp.sum(squares, axis=1, keepdims=True)
    inverse = lax.rsqrt(squares * (1.0 / width) + epsilon)
    query = (query * inverse).astype(jnp.bfloat16)
    pair = (pair * inverse).astype(jnp.bfloat16)
    entry_ref[...] = pair
    mixed = attend(query, pair, keys_ref[...], values_ref[...], visible)
    back.wait()
    store_terms(mixed, back_ref[...], terms_ref)


def next_layer_kernel(
    blocks_ref,
    first_ref,
    gain_ref,
    question_ref,
    pair_ref,
    back_ref,
    keys_ref,
    values_ref,
    visible_ref,
    terms_ref,
    entry_hbm,
    own_ref,
    entry_ref,
    sem,
):
    width = question_ref.shape[0]
    shards = lax.axis_size("tp")
    shard = lax.axis_index("tp")
    rows = first_ref.shape[0]
    share_of(whole_rows(blocks_ref, shards, shard), own_ref)
    hidden = jnp.concatenate([whole_rows(blocks_ref, shards, k) for k in range(shards)], axis=1)
    squares = lane_squares(hidden)
    scaled = (hidden * gain_ref[...].astype(jnp.float32)).astype(jnp.bfloat16)
    squares = jnp.sum(squares, axis=1, keepdims=True)
    inverse = lax.rsqrt(squares * (1.0 / width) + epsilon)
    pair = (dot(scaled, pair_ref[...]) * inverse).astype(jnp.bfloat16)
    both = jnp.where(lax.axis_index("section") == 0, first_ref[...], pair).astype(jnp.float32)
    share = entry_ref.shape[1]
    offset = shard % (shards // KV_HEADS) * share
    both = pltpu.roll(both, (2 * HEAD - offset) % (2 * HEAD), 1)
    entry_ref[...] = both[:, :share].astype(jnp.bfloat16)
    leave = pltpu.make_async_copy(entry_ref, entry_hbm, sem)
    leave.start()
    query = (dot(scaled, question_ref[...]) * inverse).astype(jnp.bfloat16)
    mixed = attend(query, pair, keys_ref[...], values_ref[...], visible_ref[...])
    store_terms(mixed, back_ref[...], terms_ref)
    leave.wait()


def in_hbm(*arrays):
    return [pltpu.with_memory_space_constraint(a, pltpu.HBM) for a in arrays]


def specs(kinds):
    spaces = {"s": pltpu.SMEM, "v": pltpu.VMEM, "h": pltpu.HBM}
    return [pl.BlockSpec(memory_space=spaces[kind]) for kind in kinds]


def first_layer(terms_shape, parents, extents, warmth, hidden, gain, question, pair, back, address, content):
    rows, width = hidden.shape
    slots = address.shape[2]
    bf16 = functools.partial(jax.ShapeDtypeStruct, dtype=jnp.bfloat16)
    return pl.pallas_call(
        first_layer_kernel,
        out_shape=(
            bf16(terms_shape),
            bf16((rows, 2 * HEAD)),
            jax.ShapeDtypeStruct(terms_shape[1:], jnp.float32),
            bf16((1, width)),
            bf16((width, HEAD)),
            bf16((width, 2 * HEAD)),
            bf16((HEAD, width)),
            bf16((rows * slots, HEAD)),
            bf16((rows * slots, HEAD)),
            jax.ShapeDtypeStruct((rows, rows * slots), jnp.int32),
            jax.ShapeDtypeStruct((rows, HEAD), jnp.float32),
        ),
        in_specs=specs("h" * 10),
        out_specs=specs("v" * 11),
        scratch_shapes=[
            pltpu.SMEM((rows,), jnp.int32),
            pltpu.SMEM((rows,), jnp.int32),
            pltpu.SMEM((rows,), jnp.float32),
            pltpu.VMEM((rows, width), jnp.bfloat16),
            pltpu.VMEM((rows, slots, HEAD), jnp.bfloat16),
            pltpu.VMEM((rows, slots, HEAD), jnp.bfloat16),
            pltpu.SemaphoreType.DMA((8,)),
            pltpu.SemaphoreType.DMA((STEPS,)),
            pltpu.SemaphoreType.DMA((STEPS,)),
        ],
        compiler_params=pltpu.CompilerParams(vmem_limit_bytes=LIMIT),
        name="first_layer",
    )(*in_hbm(parents, extents, warmth, hidden, gain, question, pair, back, address, content))


def next_layer(blocks, first, held, share):
    rows = first.shape[0]
    bf16 = functools.partial(jax.ShapeDtypeStruct, dtype=jnp.bfloat16)
    return pl.pallas_call(
        next_layer_kernel,
        out_shape=(
            bf16(blocks.shape),
            bf16((rows, share)),
            jax.ShapeDtypeStruct(blocks.shape[1:], jnp.float32),
        ),
        in_specs=specs("v" * (2 + len(held))),
        out_specs=specs("vhv"),
        scratch_shapes=[pltpu.VMEM((rows, share), jnp.bfloat16), pltpu.SemaphoreType.DMA],
        compiler_params=pltpu.CompilerParams(vmem_limit_bytes=LIMIT),
        name="next_layer",
    )(blocks, first, *held)


def stats_kernel(blocks_ref, gain_ref, warmth_ref, noise_ref, lexicon_ref, out_ref, final_ref):
    rows, width = final_ref.shape
    shards = width // HEAD
    squares = jnp.zeros((rows, HEAD), jnp.float32)
    pieces = []
    for k in range(shards):
        hidden = whole_rows(blocks_ref, shards, k)
        final_ref[:, k * HEAD : (k + 1) * HEAD] = hidden.astype(jnp.bfloat16)
        squares = squares + hidden * hidden
        pieces.append((hidden * gain_ref[k : k + 1].astype(jnp.float32)).astype(jnp.bfloat16))
    logits = dot(jnp.concatenate(pieces, axis=1), lexicon_ref[...], ((1,), (1,)))
    squares = jnp.sum(squares, axis=1, keepdims=True)
    inverse = lax.rsqrt(squares * (1.0 / width) + epsilon)
    tempered = logits * inverse / warmth_ref[:, :1]
    best = jnp.max(tempered + noise_ref[...], axis=1, keepdims=True)
    peak = jnp.max(tempered, axis=1, keepdims=True)
    mass = jnp.sum(jnp.exp(tempered - peak), axis=1, keepdims=True)
    norm = peak + jnp.log(mass)
    lane = lax.broadcasted_iota(jnp.int32, (rows, HEAD), 1)
    row = lax.broadcasted_iota(jnp.int32, (rows, HEAD), 0)
    packed = jnp.where(lane == row, best, 0.0)
    packed = jnp.where(lane == row + rows, norm, packed)
    packed = jnp.sum(packed, axis=0, keepdims=True)
    out_ref[...] = jnp.broadcast_to(packed[None], out_ref.shape)


def local_stats(blocks, gain, warmth, noise, lexicon):
    rows = warmth.shape[0]
    width = lexicon.shape[1]
    return pl.pallas_call(
        stats_kernel,
        out_shape=(
            jax.ShapeDtypeStruct((blocks.shape[0] // 8, 8, HEAD), jnp.float32),
            pltpu.VMEM((rows, width), jnp.bfloat16),
        ),
        in_specs=specs("vvvvv"),
        out_specs=tuple(specs("vv")),
        compiler_params=pltpu.CompilerParams(vmem_limit_bytes=LIMIT),
        name="local_stats",
    )(blocks, gain, warmth, noise, lexicon)


def combine_kernel(
    stats_ref, final_ref, best_hbm, norm_hbm, final_hbm, best_ref, norm_ref, sems
):
    leave = pltpu.make_async_copy(final_ref, final_hbm, sems.at[2])
    leave.start()
    rows = best_ref.shape[0]
    stats = stats_ref[...]
    highest = jnp.max(jnp.max(stats, axis=0), axis=0, keepdims=True)
    mass = jnp.sum(jnp.exp(stats - highest[None]), axis=0)
    norm = highest + jnp.log(jnp.sum(mass, axis=0, keepdims=True))
    best_ref[...] = highest[0, :rows]
    norm_ref[...] = norm[0, rows : 2 * rows]
    copies = [
        pltpu.make_async_copy(best_ref, best_hbm, sems.at[0]),
        pltpu.make_async_copy(norm_ref, norm_hbm, sems.at[1]),
    ]
    for copy in copies:
        copy.start()
    for copy in copies:
        copy.wait()
    leave.wait()


def combine(stats, final):
    rows = final.shape[0]
    row = jax.ShapeDtypeStruct((rows,), jnp.float32)
    return pl.pallas_call(
        combine_kernel,
        out_shape=(row, row, jax.ShapeDtypeStruct(final.shape, final.dtype)),
        in_specs=specs("vv"),
        out_specs=specs("hhh"),
        scratch_shapes=[
            pltpu.VMEM((rows,), jnp.float32),
            pltpu.VMEM((rows,), jnp.float32),
            pltpu.SemaphoreType.DMA((3,)),
        ],
        compiler_params=pltpu.CompilerParams(vmem_limit_bytes=LIMIT // 4),
        name="combine",
    )(stats, pltpu.with_memory_space_constraint(final, pltpu.VMEM))


def per_device(
    incoming_hidden_states,
    parent_positions,
    filled_extents,
    stored_address_tensor,
    stored_content_tensor,
    layer_scale_factors,
    question_matrix,
    address_content_matrix,
    projection_back_matrix,
    ending_scale_factors,
    lexicon_matrix,
    sampling_warmth,
    sampling_noise,
):
    shards = lax.axis_size("tp")
    sections = lax.axis_size("section")
    rows, width = incoming_hidden_states.shape
    share = address_content_matrix.shape[2] // shards
    terms_shape = (sections * shards, rows // sections, width // shards)

    def exchange(terms, own, source):
        terms = lax.all_to_all(terms, ("section", "tp"), 0, 0)
        terms = terms[source * shards : (source + 1) * shards]
        block = (own + jnp.sum(terms.astype(jnp.float32), axis=0)).astype(jnp.bfloat16)
        copies = jnp.broadcast_to(block, terms_shape)
        return lax.all_to_all(copies, ("section", "tp"), 0, 0)

    terms, first, own, *held, warmth = first_layer(
        terms_shape,
        parent_positions,
        filled_extents,
        sampling_warmth,
        incoming_hidden_states,
        layer_scale_factors,
        question_matrix,
        address_content_matrix,
        projection_back_matrix,
        stored_address_tensor,
        stored_content_tensor,
    )
    blocks = exchange(terms, own, 0)
    terms, entry, own = next_layer(blocks, first, held, share)
    blocks = exchange(terms, own, 1)
    stats, final_rows = local_stats(
        blocks,
        ending_scale_factors.reshape(width // HEAD, HEAD),
        warmth,
        sampling_noise,
        lexicon_matrix,
    )
    stats = lax.all_to_all(stats.reshape(sections * shards, 1, HEAD), ("section", "tp"), 0, 0)
    stats = stats.reshape(sections * shards // 8, 8, HEAD)
    best_score, log_norm, final_rows = combine(stats, final_rows)
    return (entry[None], final_rows, best_score, log_norm)


def solution(mesh):
    in_specs = (
        P(),
        P(),
        P(),
        P("section", None, None, None),
        P("section", None, None, None),
        P("section", None),
        P("section", None, "tp"),
        P("section", None, None),
        P("section", "tp", None),
        P(),
        P(("section", "tp"), None),
        P(),
        P(None, ("section", "tp")),
    )
    out_specs = (P("section", None, "tp"), P(), P(), P())
    return jax.shard_map(
        per_device, mesh=mesh, in_specs=in_specs, out_specs=out_specs, check_vma=False
    )
```
